256 devices in a mesh: row: 2 (over core), pitch: 32 (over z, y), rad: 4 (over x).
Axes of the slice: x: 4, y: 4, z: 8, core: 2. Of those that a mesh axis runs over, the one named last changes fastest.
Arguments:
- flow_field: float32 [2, 5, 8, 256, 4096], P('row', None, None, 'rad', 'pitch'), may hold values from -6 to 6
- inflow: float32 [2, 5, 256, 4096], P('row', None, 'rad', 'pitch'), may hold values from -6 to 6
- flux_jacobian: float32 [2, 3, 5, 5], P('row'), may hold values from -2.5 to 2.5
- sweep_jacobian: float32 [2, 2, 5, 5], P('row'), may hold values from -2.5 to 2.5
- mode_index: int32 [2, 4, 128], replicated, may hold values from -32 to 32
- destination: int32 [2, 512, 1], replicated, may hold values from 0 to 31; in each aligned block of 512 rows (0 to 511, 512 to 1023, ..., all dimensions but the last counted through in order) at most 48 rows name the same one
Outputs:
- next_flow: float32 [2, 5, 8, 256, 4096], P('row', None, None, 'rad', 'pitch')
- response: float32 [2, 32, 48, 2, 5, 256], P('row', 'pitch', None, None, None, 'rad')
The draws below stay inside these ranges and needn't reach their ends.
Inputs may be any that keep to these rules, and one draw needn't show every extreme that they name: At most 48 of one blade row's modes name the same destination, and 48 is reached in every draw.
All inputs are finite; a program needn't handle non-finite values.
Results may differ from the reference program's by a relative error of at most 0.0003.
Values sent between devices are 32-bit elements; how exact they have to be, the bound alone decides.
No kernel may reach another device: no remote copies, remote signals or barrier semaphores. Data moves between devices by JAX's collectives and lax.ppermute only.
A program may use at most 64 MiB of HBM per device.

```python
import math
import jax
import jax.numpy as jnp
import numpy as np
from jax import lax

FIELDS = 5
BLADES = 22
VANES = 54
AXIAL = 8
HARMONICS = 4
MODES_PER = 128
PITCH = 4096
RADIAL = 256
MODES = 512
CAPACITY = 48
SLOTS = 1536
N_PITCH = 32


def plant(result, own_key, least, high):
    longest = result.shape.index(max(result.shape))
    spots = []
    for shift in (0, 1):
        where = [jax.random.randint(jax.random.fold_in(own_key, axis), (), 0, length) for axis, length in enumerate(result.shape)]
        where[longest] = (where[longest] + shift) % result.shape[longest]
        spots.append(tuple(where))
    return result.at[spots[0]].set(least).at[spots[1]].set(high)


def levels(stream_key, dims, cuts, least, high):
    loudness = 1.0
    for position, blocks in cuts:
        draws = jax.random.uniform(jax.random.fold_in(jax.random.fold_in(stream_key, 6), position), (blocks,), jnp.float32, least / len(cuts), high / len(cuts))
        loudness = loudness * jnp.repeat(jnp.exp(draws), dims[position] // blocks).reshape((-1,) + (1,) * (len(dims) - 1 - position))
    return loudness


def routed_block(rng, own, number, rows, amount, top, limit, skew):
    ranking = jax.random.permutation(rng, amount)
    packed, usual = load_shares(amount, rows * top, limit, skew, True), load_shares(amount, rows * top, limit, skew, False)
    places = jnp.arange(amount)

    def named(tallies, offset_by):
        used = int((tallies > 0).sum())
        fixed = max(1, used // 4)
        moved = fixed + (places - fixed + offset_by * (used - fixed)) % max(1, amount - fixed)
        return jnp.zeros((amount,), jnp.int32).at[ranking[jnp.where(places < fixed, places, moved)]].set(jnp.asarray(tallies, jnp.int32))

    tallies = jnp.where(number % 4 == 0, named(packed, number // 4), named(usual, number - number // 4 - 1))
    mixed = jax.random.permutation(jax.random.fold_in(own, 3), amount)
    donor, sink = mixed[0:amount // 2 * 2:2], mixed[1:amount // 2 * 2:2]
    room = jnp.minimum(tallies[donor] - 1, limit - tallies[sink]) // 2
    room = jnp.where((donor == ranking[0]) | (sink == ranking[0]) | (tallies[sink] == 0), 0, jnp.maximum(room, 0))
    moved = jax.random.randint(jax.random.fold_in(own, 4), (amount // 2,), 0, 1 << 20) % (room + 1)
    tallies = tallies.at[donor].add(-moved).at[sink].add(moved)
    items = jnp.searchsorted(jnp.cumsum(tallies), jnp.arange(rows * top), side="right").astype(jnp.int32)
    grid = items.reshape(top, rows).T
    grid = grid[jax.random.permutation(jax.random.fold_in(own, 1), rows)]
    offset_by = jax.random.randint(jax.random.fold_in(own, 2), (rows, 1), 0, top)
    return jnp.take_along_axis(grid, (jnp.arange(top)[None, :] + offset_by) % top, axis=1)


def load_shares(count, total, reach, slope, full):
    loads = [(1 << 20) // math.isqrt(rank ** slope) + 1 for rank in range(1, count + 1)]
    largest = reach if full else min(reach, max(-(-total // count), total * loads[0] // sum(loads)))
    least = 1 if total - largest >= count - 1 else 0
    counts, rest = [largest] + [least] * (count - 1), total - largest - least * (count - 1)
    while rest > 0:
        candidates = [i for i in range(1, count) if counts[i] < largest] or [i for i in range(1, count) if counts[i] < reach]
        whole, remaining = sum([loads[i] for i in candidates]), rest
        for i in candidates:
            extra = min(reach - counts[i], max(1, remaining * loads[i] // whole), rest)
            counts[i] = counts[i] + extra
            rest = rest - extra
    return np.array(counts)


def noise(own_key, dims, scale, bound, split=(), kind=jnp.bfloat16):
    values = jax.random.normal(own_key, dims, jnp.float32) * scale
    if len(split) > 0:
        values = levels(own_key, dims, split, -0.22, 0.18) * values
    return jnp.clip(values, min=-bound, max=bound).astype(kind)


def setup_inputs(seed: int = 0) -> dict:
    key_of = jax.random.split(jax.random.key(seed), 7)
    flow_field = noise(key_of[0], (2, FIELDS, AXIAL, RADIAL, PITCH), 1.0, 6.0, ((0, 2), (3, 4), (4, 32)), jnp.float32)
    inflow = noise(key_of[1], (2, FIELDS, RADIAL, PITCH), 1.0, 6.0, ((0, 2), (2, 4), (3, 32)), jnp.float32)
    flux_jacobian = noise(key_of[2], (2, 3, FIELDS, FIELDS), FIELDS ** -0.5, 2.5, ((0, 2),), jnp.float32)
    sweep_jacobian = noise(key_of[3], (2, 2, FIELDS, FIELDS), FIELDS ** -0.5, 2.5, ((0, 2),), jnp.float32)
    mode_index = plant(jax.random.randint(key_of[4], (2, HARMONICS, MODES_PER), -32, 33), jax.random.fold_in(key_of[4], 1), -32, 32).astype(jnp.int32)
    destination_keys = jax.random.split(jax.random.fold_in(key_of[5], 1), 2 * MODES // MODES)
    destination_turns = jax.random.permutation(jax.random.fold_in(key_of[5], 3), 2 * MODES // MODES)
    destination = jax.vmap(lambda own, number: routed_block(jax.random.fold_in(key_of[5], 2), own, number, MODES, N_PITCH, 1, CAPACITY, 2))(destination_keys, destination_turns).reshape((2, MODES, 1))
    return {"flow_field": flow_field, "inflow": inflow, "flux_jacobian": flux_jacobian, "sweep_jacobian": sweep_jacobian, "mode_index": mode_index, "destination": destination}


PRECISE = lax.Precision.HIGHEST
FLUX_PITCH = 0.25
FLUX_RAD = 0.25
FLUX_AXIAL = 0.5
FLUX_DIFFUSE = 0.1
SWEEP_DIFFUSE = 0.5
CENTRE_WEIGHT = 2.0
RELAX = 0.7
OMEGA = 0.05
KAPPA = 2.0

def flux_step(state_now, inflow_face, jacobian, pitch_plus, pitch_minus, rad_plus, rad_minus):
    behind = jnp.concatenate([inflow_face[:, None], state_now[:, :-1]], axis=1)
    laplace = pitch_plus + pitch_minus + rad_plus + rad_minus - 4.0 * state_now
    flux_sum = FLUX_PITCH * jnp.einsum('gf,fzrp->gzrp', jacobian[0], pitch_plus - pitch_minus, precision=PRECISE)
    flux_sum = flux_sum + FLUX_RAD * jnp.einsum('gf,fzrp->gzrp', jacobian[1], rad_plus - rad_minus, precision=PRECISE)
    flux_sum = flux_sum + FLUX_AXIAL * jnp.einsum('gf,fzrp->gzrp', jacobian[2], state_now - behind, precision=PRECISE)
    return state_now - flux_sum + FLUX_DIFFUSE * laplace

def row_tables(mode_index, destination, row_id, slot_count, capacity):
    index_row = lax.dynamic_index_in_dim(mode_index, row_id, 0, keepdims=False)
    dest_row = lax.dynamic_index_in_dim(destination, row_id, 0, keepdims=False)[:, 0]
    passing = jnp.where(row_id == 0, BLADES, VANES).astype(jnp.int32)
    opposing = jnp.where(row_id == 0, VANES, BLADES).astype(jnp.int32)
    harmonic = jnp.arange(1, index_row.shape[0] + 1, dtype=jnp.int32)[:, None] * jnp.ones_like(index_row)
    orders = (harmonic * passing - index_row * opposing).reshape(-1).astype(jnp.int32)
    harmonic = harmonic.reshape(-1).astype(jnp.int32)
    mode_count = orders.shape[0]
    earlier = jnp.arange(mode_count, dtype=jnp.int32)[None, :] < jnp.arange(mode_count, dtype=jnp.int32)[:, None]
    same_dest = dest_row[None, :] == dest_row[:, None]
    rank_before = lax.optimization_barrier(jnp.sum((earlier & same_dest).astype(jnp.int32), axis=1)).astype(jnp.int32)
    target = (dest_row * capacity + rank_before).astype(jnp.int32)
    select = (target[None, :] == jnp.arange(slot_count, dtype=jnp.int32)[:, None]).astype(jnp.int32)
    slot_orders = lax.optimization_barrier(jnp.sum(select * orders[None, :], axis=1)).astype(jnp.int32)
    slot_harm = lax.optimization_barrier(jnp.sum(select * harmonic[None, :], axis=1)).astype(jnp.int32)
    filled = lax.optimization_barrier(jnp.sum(select, axis=1)).astype(jnp.int32)
    return (orders, harmonic, target, slot_orders, slot_harm, filled, select, passing)

def phase_table(orders, weights, positions, pitch_total):
    phase_index = jnp.mod(orders[:, None] * positions[None, :], pitch_total)
    angles = phase_index.astype(jnp.float32) * (2.0 * math.pi / pitch_total)
    scaling = weights.astype(jnp.float32) / math.sqrt(pitch_total)
    return (jnp.cos(angles) * scaling[:, None], -jnp.sin(angles) * scaling[:, None])

def transform(cosine, sine_part, exit_face):
    real_part = jnp.einsum('sp,cp->sc', cosine, exit_face, precision=PRECISE)
    imag_part = jnp.einsum('sp,cp->sc', sine_part, exit_face, precision=PRECISE)
    return jnp.stack([real_part, imag_part], axis=1)

def wrapped(orders, pitch_total):
    return jnp.mod(orders + pitch_total // 2, pitch_total) - pitch_total // 2

def operate(widened, freq_term, wave_term, twist_map, radial):
    centre = widened[..., 1:-1]
    outer_side = widened[..., 2:]
    inner_side = widened[..., :-2]
    turned_re = jnp.einsum('gf,sfr->sgr', twist_map, centre[:, 0], precision=PRECISE)
    turned_im = jnp.einsum('gf,sfr->sgr', twist_map, centre[:, 1], precision=PRECISE)
    grade_re = jnp.einsum('gf,sfr->sgr', radial, outer_side[:, 0] - inner_side[:, 0], precision=PRECISE)
    grade_im = jnp.einsum('gf,sfr->sgr', radial, outer_side[:, 1] - inner_side[:, 1], precision=PRECISE)
    sig_col = freq_term[:, None, None]
    wave_col = wave_term[:, None, None]
    out_re = CENTRE_WEIGHT * centre[:, 0] - SWEEP_DIFFUSE * (outer_side[:, 0] + inner_side[:, 0]) - sig_col * centre[:, 1] - wave_col * turned_im + 0.5 * grade_re
    out_im = CENTRE_WEIGHT * centre[:, 1] - SWEEP_DIFFUSE * (outer_side[:, 1] + inner_side[:, 1]) + sig_col * centre[:, 0] + wave_col * turned_re + 0.5 * grade_im
    return (out_re, out_im)

def relax_step(centre, target, applied, freq_term):
    resid_real = target[:, 0] - applied[0]
    resid_imag = target[:, 1] - applied[1]
    sig_col = freq_term[:, None, None]
    denominator = CENTRE_WEIGHT * CENTRE_WEIGHT + sig_col * sig_col
    new_re = centre[:, 0] + RELAX * (CENTRE_WEIGHT * resid_real + sig_col * resid_imag) / denominator
    new_im = centre[:, 1] + RELAX * (CENTRE_WEIGHT * resid_imag - sig_col * resid_real) / denominator
    return jnp.stack([new_re, new_im], axis=1)

def reference(flow_field, inflow, flux_jacobian, sweep_jacobian, mode_index, destination):
    positions = jnp.arange(PITCH, dtype=jnp.int32)
    flows = []
    placed_rows = []
    tables = []
    for row_id in range(2):
        state_now = flow_field[row_id]
        zero_plane = jnp.zeros_like(state_now[:, :, :1])
        rad_plus = jnp.concatenate([state_now[:, :, 1:], zero_plane], axis=2)
        rad_minus = jnp.concatenate([zero_plane, state_now[:, :, :-1]], axis=2)
        next_state = flux_step(state_now, inflow[row_id], flux_jacobian[row_id], jnp.roll(state_now, -1, 3), jnp.roll(state_now, 1, 3), rad_plus, rad_minus)
        flows.append(next_state)
        exit_face = next_state[:, -1].reshape(FIELDS * RADIAL, PITCH)
        info = row_tables(mode_index, destination, row_id, SLOTS, CAPACITY)
        cosine, sine_part = phase_table(info[0], jnp.ones((MODES,), jnp.int32), positions, PITCH)
        modal = transform(cosine, sine_part, exit_face)
        placed = jnp.zeros((SLOTS, 2, FIELDS * RADIAL), jnp.float32).at[info[2]].set(modal)
        placed_rows.append(placed)
        tables.append(info)
    answers = []
    for receiver in range(2):
        source_row = 1 - receiver
        info = tables[source_row]
        amplitude = placed_rows[source_row].reshape(SLOTS, 2, FIELDS, RADIAL)
        freq_term = OMEGA * info[4].astype(jnp.float32) * info[7].astype(jnp.float32)
        wave_term = KAPPA * wrapped(info[3], PITCH).astype(jnp.float32) / PITCH
        current = amplitude
        for repeat_no in range(2):
            widened = jnp.pad(current, ((0, 0), (0, 0), (0, 0), (1, 1)))
            applied = operate(widened, freq_term, wave_term, sweep_jacobian[receiver, 0], sweep_jacobian[receiver, 1])
            current = relax_step(current, amplitude, applied, freq_term)
        answers.append(current.reshape(N_PITCH, CAPACITY, 2, FIELDS, RADIAL))
    return (jnp.stack(flows, axis=0), jnp.stack(answers, axis=0))
```

```python
import math

import jax
import jax.numpy as jnp
import ml_dtypes
import numpy as np
from jax import lax
from jax.experimental import pallas as pl
from jax.experimental.pallas import tpu as pltpu
from jax.sharding import PartitionSpec as P

F = 5
BLADES = 22
VANES = 54
AXIAL = 8
HARMONICS = 4
MODES_PER = 128
MODES = 512
PITCH = 4096
K_MAX = 32
CAPACITY = 48
N_PITCH = 32
N_RAD = 4
RAD = 64
LANES = 128
GROUPS = 3
TABLE = GROUPS * LANES
SLOT_LANES = 64
PACKED = N_PITCH * SLOT_LANES

FLUX_PITCH = 0.25
FLUX_RAD = 0.25
FLUX_AXIAL = 0.5
FLUX_DIFFUSE = 0.1
RELAX = 0.7
OMEGA = 0.05
KAPPA = 2.0

f32 = jnp.float32
bf16 = jnp.bfloat16
SMEM = pl.BlockSpec(memory_space=pltpu.SMEM)
VMEM = pl.BlockSpec(memory_space=pltpu.VMEM)


def iota(shape, dim):
    return lax.broadcasted_iota(jnp.int32, shape, dim)


def fourier_tables():
    weights = np.zeros((2, GROUPS, 3 * 2 * LANES, 2 * LANES), np.float64)
    codes = np.full((2, 8, TABLE), -1, np.int32)
    j = np.arange(LANES)
    for b, (own, other) in enumerate(((BLADES, VANES), (VANES, BLADES))):
        used = [0] * GROUPS
        for n in range(1, HARMONICS + 1):
            for k in range(-K_MAX, K_MAX + 1):
                q = (n * own - k * other) // 2
                t = q % 16
                part = min(t, 16 - t)
                sign = 1.0 if t <= 8 else -1.0
                group, member = divmod(part, 3)
                lane = used[group]
                used[group] += 1
                angle = 2.0 * np.pi * ((q * j) % 2048) / 2048.0
                cos, sin = np.cos(angle) / 64.0, np.sin(angle) / 64.0
                rows = weights[b, group, member * 256 : member * 256 + 256]
                rows[:LANES, lane] = cos
                rows[LANES:, lane] = sign * sin
                rows[:LANES, LANES + lane] = -sin
                rows[LANES:, LANES + lane] = sign * cos
                codes[b, :, group * LANES + lane] = n * 128 + k + K_MAX
    high = weights.astype(ml_dtypes.bfloat16)
    low = (weights - high.astype(np.float64)).astype(ml_dtypes.bfloat16)
    return np.stack([high, low], axis=1), codes


def mix(jac, k, g, parts):
    total = jac[0, k, g, 0] * parts[0]
    for f in range(1, F):
        total = total + jac[0, k, g, f] * parts[f]
    return total


def exit_kernel(jac, flow, out):
    now = [flow[0, f, 1] for f in range(F)]
    behind = [flow[0, f, 0] for f in range(F)]
    lane = iota((RAD, LANES), 1)
    row = iota((RAD, LANES), 0)
    change = [now[f] - behind[f] for f in range(F)]
    edges = jnp.zeros((RAD, LANES), f32)
    out[...] = jnp.zeros(out.shape, f32)
    for g in range(F):
        pitch = FLUX_PITCH * mix(jac, 0, g, now)
        radial = FLUX_RAD * mix(jac, 1, g, now)
        soft = FLUX_DIFFUSE * now[g]
        to_low, to_high = soft - pitch, soft + pitch
        inward, outward = soft - radial, soft + radial
        value = now[g] - FLUX_AXIAL * mix(jac, 2, g, change) - 4.0 * soft
        value = value + jnp.where(lane == LANES - 1, 0.0, pltpu.roll(to_low, LANES - 1, 1))
        value = value + jnp.where(lane == 0, 0.0, pltpu.roll(to_high, 1, 1))
        value = value + jnp.where(row == RAD - 1, 0.0, pltpu.roll(inward, RAD - 1, 0))
        value = value + jnp.where(row == 0, 0.0, pltpu.roll(outward, 1, 0))
        out[:, g, :] = value
        edges = jnp.where(lane == g, pltpu.roll(to_low, g, 1) if g else to_low, edges)
        edges = jnp.where(lane == 8 + g, pltpu.roll(to_high, 9 + g, 1), edges)
        out[g, 6:7, :] = inward[0:1]
        out[F + g, 6:7, :] = outward[RAD - 1 : RAD]
    out[:, 5, :] = edges


def halo_kernel(flow, to_low, to_high, first, last):
    lane = iota((RAD, LANES), 1)
    low = jnp.zeros((RAD, LANES), f32)
    high = jnp.zeros((RAD, LANES), f32)
    for f in range(F):
        for z in range(AXIAL):
            k = f * AXIAL + z
            block = flow[0, f, z]
            low = jnp.where(lane == k, pltpu.roll(block, k, 1) if k else block, low)
            high = jnp.where(lane == k, pltpu.roll(block, k + 1, 1), high)
            first[f, z : z + 1, :] = block[0:1]
            last[f, z : z + 1, :] = block[RAD - 1 : RAD]
    to_low[...] = low
    to_high[...] = high


def flux_kernel(jac, flow, inflow, next_column, last_column, next_row, last_row, out, previous):
    z = pl.program_id(0)
    lane = iota((RAD, LANES), 1)
    row = iota((RAD, LANES), 0)

    @pl.when(z == 0)
    def _():
        previous[...] = inflow[0]

    now, pitch, radial, change, laplace = [], [], [], [], []
    for f in range(F):
        block = flow[0, f, 0]
        k = f * AXIAL + z
        right = pltpu.roll(next_column[...], LANES - 1 - k, 1)
        left = pltpu.roll(last_column[...], lax.bitwise_and(LANES - k, LANES - 1), 1)
        right = jnp.where(lane == LANES - 1, right, pltpu.roll(block, LANES - 1, 1))
        left = jnp.where(lane == 0, left, pltpu.roll(block, 1, 1))
        above = jnp.where(row == RAD - 1, next_row[f, pl.ds(z, 1), :], pltpu.roll(block, RAD - 1, 0))
        below = jnp.where(row == 0, last_row[f, pl.ds(z, 1), :], pltpu.roll(block, 1, 0))
        now.append(block)
        pitch.append(FLUX_PITCH * (right - left))
        radial.append(FLUX_RAD * (above - below))
        change.append(FLUX_AXIAL * (block - previous[f]))
        laplace.append(FLUX_DIFFUSE * (right + left + above + below - 4.0 * block))
    for g in range(F):
        flux = mix(jac, 0, g, pitch) + mix(jac, 1, g, radial) + mix(jac, 2, g, change)
        out[0, g, 0] = now[g] - flux + laplace[g]
    for f in range(F):
        previous[f] = now[f]


def table_kernel(ids, dest, modes, codes, place, terms):
    source = 1 - ids[0]
    own = jnp.where(source == 0, BLADES, VANES)
    other = jnp.where(source == 0, VANES, BLADES)
    dest_row = dest[pl.ds(source, 1), :]
    listed = modes[source]
    code_row = jnp.concatenate(
        [listed[h : h + 1] + (K_MAX + 128 * (h + 1)) for h in range(HARMONICS)], axis=1
    )

    def column(row, block):
        part = row[:, block * LANES : (block + 1) * LANES]
        return jnp.transpose(jnp.broadcast_to(part, (LANES, LANES)))

    here = iota((LANES, LANES), 0)
    there = iota((LANES, LANES), 1)
    spread = iota((LANES, PACKED), 1)
    target = ids[1] * SLOT_LANES + lax.bitwise_and(there, SLOT_LANES - 1)
    slot_code = jnp.zeros((1, LANES), jnp.int32)
    hits = []
    for block in range(MODES // LANES):
        dest_col = column(dest_row, block)
        before = jnp.zeros((LANES, LANES), f32)
        for past in range(block + 1):
            same = dest_col == dest_row[:, past * LANES : (past + 1) * LANES]
            if past == block:
                same = same & (there < here)
            before = before + same.astype(f32)
        rank = jnp.sum(before, axis=1, keepdims=True).astype(jnp.int32)
        slot = dest_col * SLOT_LANES + rank
        hits.append((slot[:, :1] == spread).astype(f32).astype(bf16))
        mine = jnp.where(slot == target, column(code_row, block), 0)
        slot_code = slot_code + jnp.sum(mine, axis=0, keepdims=True)
    hit = jnp.concatenate(hits, axis=0)
    code_table = codes[source]
    lane_code = jnp.concatenate([column(code_table[0:1], g) for g in range(GROUPS)], axis=0)
    listed_at = (lane_code[:, :1] == code_row).astype(f32).astype(bf16)
    place[...] = jnp.dot(listed_at, hit, preferred_element_type=f32).astype(bf16)
    n = lax.shift_right_logical(slot_code, 7)
    m = n * own - (lax.bitwise_and(slot_code, 127) - K_MAX) * other
    m = jnp.where(n > 0, m, 0)
    wave = lax.bitwise_and(m + PITCH // 2, PITCH - 1) - PITCH // 2
    sigma = OMEGA * n.astype(f32) * own.astype(f32)
    kappa = KAPPA * wave.astype(f32) / PITCH
    lane = iota((1, LANES), 1)
    sign = jnp.where(lane < SLOT_LANES, -1.0, 1.0)
    terms[...] = jnp.zeros(terms.shape, f32)
    terms[0:1] = sign * sigma
    terms[1:2] = sign * kappa
    terms[2:3] = RELAX / (4.0 + sigma * sigma)


def transform_kernel(cells, weights, out):
    lane = iota((8, LANES), 1)
    sub = iota((8, LANES), 0)
    parts = []
    for half in range(2):
        x = [cells[2 * p + half] for p in range(N_PITCH)]
        z = [x[p] + x[p + 16] for p in range(16)]
        even = [None] + [z[p] + z[16 - p] for p in range(1, 8)]
        odd = [None] + [z[p] - z[16 - p] for p in range(1, 8)]
        columns = []
        for t in range(9):
            re = z[0] + z[8] if t % 2 == 0 else z[0] - z[8]
            im = jnp.zeros((8, LANES), f32)
            for p in range(1, 8):
                re = re + math.cos(2.0 * math.pi * ((t * p) % 16) / 16) * even[p]
                if t % 8:
                    im = im - math.sin(2.0 * math.pi * ((t * p) % 16) / 16) * odd[p]

            def edge(value, offset):
                spread = jnp.broadcast_to(value[5:6, :], (8, LANES))
                return jnp.sum(jnp.where(lane == sub + offset, spread, 0.0), axis=1, keepdims=True)

            cos, sin = math.cos(2.0 * math.pi * t / 16), math.sin(2.0 * math.pi * t / 16)
            low_re, high_re = edge(re, 0), edge(re, 8)
            low_im, high_im = (edge(im, 0), edge(im, 8)) if t % 8 else (0.0, 0.0)
            re = re + jnp.where(lane == LANES - 1, cos * low_re - sin * low_im, 0.0)
            re = re + jnp.where(lane == 0, cos * high_re + sin * high_im, 0.0)
            im = im + jnp.where(lane == LANES - 1, cos * low_im + sin * low_re, 0.0)
            im = im + jnp.where(lane == 0, cos * high_im - sin * high_re, 0.0)
            columns += [re, im]
        parts.append(columns)
    for group in range(GROUPS):
        left = jnp.concatenate(
            [
                jnp.concatenate([parts[half][group * 6 + i] for i in range(6)], axis=1)
                for half in range(2)
            ],
            axis=0,
        )
        high = left.astype(bf16)
        low = (left - high.astype(f32)).astype(bf16)
        both = jnp.dot(
            jnp.concatenate([high, low], axis=0), weights[0, group], preferred_element_type=f32
        )
        value = both[:16] + both[16:]
        value = value + jnp.dot(high, weights[1, group], preferred_element_type=f32)
        out[0:16, group * LANES : (group + 1) * LANES] = value[:, :LANES]
        out[16:32, group * LANES : (group + 1) * LANES] = value[:, LANES:]


def place_kernel(values, place, out):
    x = values[...]
    high = x.astype(bf16)
    rest = x - high.astype(f32)
    mid = rest.astype(bf16)
    low = (rest - mid.astype(f32)).astype(bf16)
    split = jnp.concatenate([high, mid, low], axis=0)
    lane = iota((8, LANES), 1)
    for pair in range(N_PITCH // 2):
        picked = jnp.dot(
            split, place[:, pair * LANES : (pair + 1) * LANES], preferred_element_type=f32
        )
        picked = picked[0:32] + picked[32:64] + picked[64:96]
        for half in range(2):
            re, im = picked[half * 8 : half * 8 + 8], picked[16 + half * 8 : 24 + half * 8]
            out[4 * pair + half] = jnp.where(lane < SLOT_LANES, re, pltpu.roll(im, SLOT_LANES, 1))
            out[4 * pair + 2 + half] = jnp.where(
                lane < SLOT_LANES, pltpu.roll(re, SLOT_LANES, 1), im
            )


SPAN = RAD + 8


def sweep_kernel(ids, jac, modes, terms, main, low, high):
    rad = ids[0]
    radius = iota((SPAN, LANES), 0) - 4
    inside = jnp.where(
        ((radius < 0) & (rad == 0)) | ((radius >= RAD) & (rad == N_RAD - 1)), 0.0, 1.0
    )
    sigma, kappa, scale = terms[0:1], terms[1:2], terms[2:3]
    index = iota((8, LANES), 0)

    def turned(value):
        return pltpu.roll(value, SLOT_LANES, 1)

    start = []
    for f in range(F):
        before = jnp.where(index == 3, modes[f, 6:7, :], 0.0)
        after = jnp.where(index == 4, modes[F + f, 6:7, :], 0.0)
        body = jnp.concatenate([before[:4], modes[:, f, :], after[4:]], axis=0)
        start.append(body * inside)
    current = start
    for _ in range(2):
        above = [pltpu.roll(w, SPAN - 1, 0) for w in current]
        below = [pltpu.roll(w, 1, 0) for w in current]
        grade = [above[f] - below[f] for f in range(F)]
        update = []
        for g in range(F):
            w = current[g]
            applied = 2.0 * w - 0.5 * (above[g] + below[g]) + sigma * turned(w)
            applied = applied + kappa * turned(mix(jac, 0, g, current))
            applied = applied + 0.5 * mix(jac, 1, g, grade)
            rest = start[g] - applied
            update.append((w + scale * (2.0 * rest - sigma * turned(rest))) * inside)
        current = update
    for f in range(F):
        main[f] = current[f][4 : 4 + RAD]
        low[f] = current[f][:8]
        high[f] = current[f][SPAN - 8 :]


def finish_kernel(main, from_low, from_high, out):
    index = iota((8, LANES), 0)
    for f in range(F):
        first = main[f, 0:8] + jnp.where(index < 4, pltpu.roll(from_low[f], 4, 0), 0.0)
        last = main[f, RAD - 8 :] + jnp.where(index >= 4, pltpu.roll(from_high[f], 4, 0), 0.0)
        body = jnp.concatenate([first, main[f, 8 : RAD - 8], last], axis=0)
        turned = jnp.transpose(body)
        out[0, 0, :, 0, f, :] = turned[:CAPACITY]
        out[0, 0, :, 1, f, :] = turned[SLOT_LANES : SLOT_LANES + CAPACITY]


def shape(*dims, dtype=f32):
    return jax.ShapeDtypeStruct(dims, dtype)


def cost(flops, size):
    return pl.CostEstimate(flops=flops, bytes_accessed=size, transcendentals=0)


BIG = pltpu.CompilerParams(vmem_limit_bytes=40 * 1024 * 1024)


def on_device(flow, inflow, flux_jacobian, sweep_jacobian, mode_index, destination):
    weights, codes = fourier_tables()
    row = lax.axis_index("row")
    pitch = lax.axis_index("pitch")
    rad = lax.axis_index("rad")

    face = pl.pallas_call(
        exit_kernel,
        grid=(1,),
        out_shape=shape(RAD, 8, LANES),
        in_specs=[SMEM, pl.BlockSpec((1, F, 2, RAD, LANES), lambda i: (0, 0, 3, 0, 0))],
        out_specs=pl.BlockSpec((RAD, 8, LANES), lambda i: (0, 0, 0)),
        compiler_params=BIG,
        cost_estimate=cost(4_000_000, 600_000),
    )(flux_jacobian, flow)
    cells = lax.all_to_all(face, "pitch", 0, 0, tiled=True)

    ids = jnp.stack([row, pitch]).astype(jnp.int32)
    place, terms = pl.pallas_call(
        table_kernel,
        out_shape=(shape(TABLE, PACKED, dtype=bf16), shape(8, LANES)),
        in_specs=[SMEM, VMEM, VMEM, VMEM],
        out_specs=(VMEM, VMEM),
        compiler_params=BIG,
        cost_estimate=cost(2 * TABLE * MODES * PACKED, 2_000_000),
    )(ids, destination[:, :, 0], mode_index, codes)

    to_low, to_high, first, last = pl.pallas_call(
        halo_kernel,
        out_shape=(shape(RAD, LANES), shape(RAD, LANES), shape(F, AXIAL, LANES), shape(F, AXIAL, LANES)),
        in_specs=[VMEM],
        out_specs=(VMEM,) * 4,
        compiler_params=BIG,
        cost_estimate=cost(4_000_000, 1_400_000),
    )(flow)
    up = [(i, (i + 1) % N_PITCH) for i in range(N_PITCH)]
    down = [((i + 1) % N_PITCH, i) for i in range(N_PITCH)]
    outward = [(i, i + 1) for i in range(N_RAD - 1)]
    inward = [(i + 1, i) for i in range(N_RAD - 1)]
    next_column = lax.ppermute(to_low, "pitch", down)
    last_column = lax.ppermute(to_high, "pitch", up)
    next_row = lax.ppermute(first, "rad", inward)
    last_row = lax.ppermute(last, "rad", outward)

    next_flow = pl.pallas_call(
        flux_kernel,
        grid=(AXIAL,),
        out_shape=shape(1, F, AXIAL, RAD, LANES),
        in_specs=[
            SMEM,
            pl.BlockSpec((1, F, 1, RAD, LANES), lambda z: (0, 0, z, 0, 0)),
            pl.BlockSpec((1, F, RAD, LANES), lambda z: (0, 0, 0, 0)),
            pl.BlockSpec((RAD, LANES), lambda z: (0, 0)),
            pl.BlockSpec((RAD, LANES), lambda z: (0, 0)),
            pl.BlockSpec((F, AXIAL, LANES), lambda z: (0, 0, 0)),
            pl.BlockSpec((F, AXIAL, LANES), lambda z: (0, 0, 0)),
        ],
        out_specs=pl.BlockSpec((1, F, 1, RAD, LANES), lambda z: (0, 0, z, 0, 0)),
        scratch_shapes=[pltpu.VMEM((F, RAD, LANES), f32)],
        compiler_params=BIG,
        cost_estimate=cost(20_000_000, 3_000_000),
    )(flux_jacobian, flow, inflow, next_column, last_column, next_row, last_row)

    own_weights = lax.dynamic_index_in_dim(jnp.asarray(weights), row, 0, keepdims=False)
    modes = pl.pallas_call(
        transform_kernel,
        out_shape=shape(32, TABLE),
        in_specs=[VMEM, VMEM],
        out_specs=VMEM,
        compiler_params=BIG,
        cost_estimate=cost(60_000_000, 3_000_000),
    )(cells, own_weights)
    modes = lax.ppermute(modes, "row", [(0, 1), (1, 0)])
    placed = pl.pallas_call(
        place_kernel,
        out_shape=shape(RAD, 8, LANES),
        in_specs=[VMEM, VMEM],
        out_specs=VMEM,
        compiler_params=BIG,
        cost_estimate=cost(150_000_000, 2_000_000),
    )(modes, place)
    amplitude = lax.all_to_all(placed, "pitch", 0, 0, tiled=True)
    main, low, high = pl.pallas_call(
        sweep_kernel,
        out_shape=(shape(F, RAD, LANES), shape(F, 8, LANES), shape(F, 8, LANES)),
        in_specs=[SMEM, SMEM, VMEM, VMEM],
        out_specs=(VMEM,) * 3,
        compiler_params=BIG,
        cost_estimate=cost(8_000_000, 500_000),
    )(rad.astype(jnp.int32).reshape(1), sweep_jacobian, amplitude, terms)
    from_high = lax.ppermute(low, "rad", inward)
    from_low = lax.ppermute(high, "rad", outward)
    response = pl.pallas_call(
        finish_kernel,
        out_shape=shape(1, 1, CAPACITY, 2, F, RAD),
        in_specs=[VMEM] * 3,
        out_specs=VMEM,
        compiler_params=BIG,
        cost_estimate=cost(1_000_000, 800_000),
    )(main, from_low, from_high)
    return next_flow, response


def solution(mesh):
    placed = (
        P("row", None, None, "rad", "pitch"),
        P("row", None, "rad", "pitch"),
        P("row", None, None, None),
        P("row", None, None, None),
        P(),
        P(),
    )
    return jax.shard_map(
        on_device,
        mesh=mesh,
        in_specs=placed,
        out_specs=(
            P("row", None, None, "rad", "pitch"),
            P("row", "pitch", None, None, None, "rad"),
        ),
        check_vma=False,
    )
```

```python
import math

import jax
import jax.numpy as jnp
import ml_dtypes
import numpy as np
from jax import lax
from jax.experimental import pallas as pl
from jax.experimental.pallas import tpu as pltpu
from jax.sharding import PartitionSpec as P

F = 5
BLADES = 22
VANES = 54
AXIAL = 8
HARMONICS = 4
MODES_PER = 128
MODES = 512
PITCH = 4096
K_MAX = 32
CAPACITY = 48
N_PITCH = 32
N_RAD = 4
RAD = 64
LANES = 128
GROUPS = 3
TABLE = GROUPS * LANES
SLOT_LANES = 64
PACKED = N_PITCH * SLOT_LANES

FLUX_PITCH = 0.25
FLUX_RAD = 0.25
FLUX_AXIAL = 0.5
FLUX_DIFFUSE = 0.1
RELAX = 0.7
OMEGA = 0.05
KAPPA = 2.0

f32 = jnp.float32
bf16 = jnp.bfloat16
SMEM = pl.BlockSpec(memory_space=pltpu.SMEM)
VMEM = pl.BlockSpec(memory_space=pltpu.VMEM)


def iota(shape, dim):
    return lax.broadcasted_iota(jnp.int32, shape, dim)


CLASS_LANES = 43
HALF_CLASS = 22


def fourier_tables():
    weights = np.zeros((2, 2, 9, LANES, LANES), np.float64)
    codes = np.full((2, 8, TABLE), -1, np.int32)
    j = np.arange(LANES)
    for b, (own, other) in enumerate(((BLADES, VANES), (VANES, BLADES))):
        used = np.zeros((9, 2), int)
        for n in range(1, HARMONICS + 1):
            for k in range(-K_MAX, K_MAX + 1):
                q = (n * own - k * other) // 2
                t = q % 16
                part, side = (t, 0) if t <= 8 else (16 - t, 1)
                lane = side * HALF_CLASS + used[part, side]
                used[part, side] += 1
                angle = 2.0 * np.pi * ((q * j) % 2048) / 2048.0
                weights[b, 0, part, :, lane] = np.cos(angle) / 64.0
                weights[b, 0, part, :, SLOT_LANES + lane] = np.sin(angle) / 64.0
                group, member = divmod(part, 3)
                codes[b, :, group * LANES + member * CLASS_LANES + lane] = n * 128 + k + K_MAX
        assert used.max() <= HALF_CLASS - 1
    high = weights[:, 0].astype(ml_dtypes.bfloat16)
    low = (weights[:, 0] - high.astype(np.float64)).astype(ml_dtypes.bfloat16)
    return np.stack([high, low], axis=1), codes


def mix(coefficients, parts):
    total = coefficients[0] * parts[0]
    for f in range(1, F):
        total = total + coefficients[f] * parts[f]
    return total


def flux_row(jac, k, g):
    return [jac[k, g, 0, f] for f in range(F)]


def sweep_row(jac, k, g):
    return [jac[0, g, k, f] for f in range(F)]


def exit_kernel(jacobian, flow, out, planes, jac, arrived):
    copies = [
        pltpu.make_async_copy(flow.at[0, f, pl.ds(AXIAL - 2, 2)], planes.at[f], arrived.at[f])
        for f in range(F)
    ]
    copies.append(pltpu.make_async_copy(jacobian, jac, arrived.at[F]))
    for copy in copies:
        copy.start()
    for copy in copies:
        copy.wait()
    now = [planes[f, 1] for f in range(F)]
    behind = [planes[f, 0] for f in range(F)]
    lane = iota((RAD, LANES), 1)
    row = iota((RAD, LANES), 0)
    change = [now[f] - behind[f] for f in range(F)]
    edges = jnp.zeros((RAD, LANES), f32)
    out[...] = jnp.zeros(out.shape, f32)
    for g in range(F):
        pitch = mix([FLUX_PITCH * c for c in flux_row(jac, 0, g)], now)
        radial = mix([FLUX_RAD * c for c in flux_row(jac, 1, g)], now)
        soft = FLUX_DIFFUSE * now[g]
        to_low, to_high = soft - pitch, soft + pitch
        inward, outward = soft - radial, soft + radial
        value = now[g] - mix([FLUX_AXIAL * c for c in flux_row(jac, 2, g)], change) - 4.0 * soft
        value = value + jnp.where(lane == LANES - 1, 0.0, pltpu.roll(to_low, LANES - 1, 1))
        value = value + jnp.where(lane == 0, 0.0, pltpu.roll(to_high, 1, 1))
        value = value + jnp.where(row == RAD - 1, 0.0, pltpu.roll(inward, RAD - 1, 0))
        value = value + jnp.where(row == 0, 0.0, pltpu.roll(outward, 1, 0))
        out[:, g, :] = value
        edges = jnp.where(lane == g, pltpu.roll(to_low, g, 1) if g else to_low, edges)
        edges = jnp.where(lane == 8 + g, pltpu.roll(to_high, 9 + g, 1), edges)
        out[g, 6:7, :] = inward[0:1]
        out[F + g, 6:7, :] = outward[RAD - 1 : RAD]
    out[:, 5, :] = edges


def halo_kernel(flow, pitch_near, pitch_far, rad_near, rad_far):
    lane = iota((RAD, LANES), 1)
    low = jnp.zeros((RAD, LANES), f32)
    high = jnp.zeros((RAD, LANES), f32)
    pitch_even = lax.rem(lax.axis_index("pitch"), 2) == 0
    rad_even = lax.rem(lax.axis_index("rad"), 2) == 0
    for f in range(F):
        for z in range(AXIAL):
            k = f * AXIAL + z
            block = flow[0, f, z]
            low = jnp.where(lane == k, pltpu.roll(block, k, 1) if k else block, low)
            high = jnp.where(lane == k, pltpu.roll(block, k + 1, 1), high)
            first, last = block[0:1], block[RAD - 1 : RAD]
            rad_near[f, z : z + 1, :] = jnp.where(rad_even, last, first)
            rad_far[f, z : z + 1, :] = jnp.where(rad_even, first, last)
    pitch_near[...] = jnp.where(pitch_even, high, low)
    pitch_far[...] = jnp.where(pitch_even, low, high)


DEPTH = 4
ROWS = 16


def flux_kernel(jac, flow, inflow, pitch_near, pitch_far, rad_near, rad_far, after, out, done, previous):
    step = pl.program_id(0)
    lane = iota((ROWS, LANES), 1)
    row = iota((ROWS, LANES), 0)
    pitch_even = lax.rem(lax.axis_index("pitch"), 2) == 0
    rad_even = lax.rem(lax.axis_index("rad"), 2) == 0

    @pl.when(step == 0)
    def _():
        previous[...] = inflow[0]

    pitch_jac = [[FLUX_PITCH * c for c in flux_row(jac, 0, g)] for g in range(F)]
    rad_jac = [[FLUX_RAD * c for c in flux_row(jac, 1, g)] for g in range(F)]
    axial_jac = [[FLUX_AXIAL * c for c in flux_row(jac, 2, g)] for g in range(F)]
    for z in range(DEPTH):
        axial = step * DEPTH + z
        for start in range(0, RAD, ROWS):
            rows = slice(start, start + ROWS)
            near, far = pitch_near[rows], pitch_far[rows]
            next_column = jnp.where(pitch_even, near, far)
            last_column = jnp.where(pitch_even, far, near)
            now, pitch, radial, change, total = [], [], [], [], []
            for f in range(F):
                block = flow[0, f, z, rows]
                k = f * AXIAL + axial
                right = pltpu.roll(next_column, LANES - 1 - k, 1)
                left = pltpu.roll(last_column, lax.bitwise_and(LANES - k, LANES - 1), 1)
                right = jnp.where(lane == LANES - 1, right, pltpu.roll(block, LANES - 1, 1))
                left = jnp.where(lane == 0, left, pltpu.roll(block, 1, 1))
                if start + ROWS < RAD:
                    above = flow[0, f, z, start + 1 : start + ROWS + 1]
                else:
                    edge_near, edge_far = rad_near[f, pl.ds(axial, 1), :], rad_far[f, pl.ds(axial, 1), :]
                    edge = jnp.where(rad_even, edge_near, edge_far)
                    above = jnp.where(row == ROWS - 1, edge, pltpu.roll(block, ROWS - 1, 0))
                if start:
                    below = flow[0, f, z, start - 1 : start + ROWS - 1]
                else:
                    edge_near, edge_far = rad_near[f, pl.ds(axial, 1), :], rad_far[f, pl.ds(axial, 1), :]
                    edge = jnp.where(rad_even, edge_far, edge_near)
                    below = jnp.where(row == 0, edge, pltpu.roll(block, 1, 0))
                behind = flow[0, f, z - 1, rows] if z else previous[f, rows]
                now.append(block)
                pitch.append(right - left)
                radial.append(above - below)
                change.append(block - behind)
                total.append((right + left) + (above + below))
            for g in range(F):
                flux = mix(pitch_jac[g], pitch) + mix(rad_jac[g], radial) + mix(axial_jac[g], change)
                soft = (1.0 - 4.0 * FLUX_DIFFUSE) * now[g] + FLUX_DIFFUSE * total[g]
                out[0, g, z, rows] = soft - flux
    for f in range(F):
        previous[f] = flow[0, f, DEPTH - 1]
    done[...] = jnp.zeros(done.shape, f32)


def table_kernel(dest, modes, codes, place, terms):
    source = 1 - lax.axis_index("row")
    own = jnp.where(source == 0, BLADES, VANES)
    other = jnp.where(source == 0, VANES, BLADES)
    dest_row = dest[source]
    listed = modes[source]
    code_row = jnp.concatenate(
        [listed[h : h + 1] + (K_MAX + 128 * (h + 1)) for h in range(HARMONICS)], axis=1
    )

    def column(row, block):
        part = row[:, block * LANES : (block + 1) * LANES]
        return jnp.transpose(jnp.broadcast_to(part, (LANES, LANES)))

    here = iota((LANES, LANES), 0)
    there = iota((LANES, LANES), 1)
    spread = iota((LANES, PACKED), 1)
    target = lax.axis_index("pitch") * SLOT_LANES + lax.bitwise_and(there, SLOT_LANES - 1)
    slot_code = jnp.zeros((1, LANES), jnp.int32)
    hits = []
    for block in range(MODES // LANES):
        dest_col = column(dest_row, block)
        before = jnp.zeros((LANES, LANES), f32)
        for past in range(block + 1):
            same = dest_col == dest_row[:, past * LANES : (past + 1) * LANES]
            if past == block:
                same = same & (there < here)
            before = before + same.astype(f32)
        rank = jnp.sum(before, axis=1, keepdims=True).astype(jnp.int32)
        slot = dest_col * SLOT_LANES + rank
        hits.append((slot[:, :1] == spread).astype(f32).astype(bf16))
        mine = jnp.where(slot == target, column(code_row, block), 0)
        slot_code = slot_code + jnp.sum(mine, axis=0, keepdims=True)
    hit = jnp.concatenate(hits, axis=0)
    code_table = codes[source]
    lane_code = jnp.concatenate([column(code_table[0:1], g) for g in range(GROUPS)], axis=0)
    listed_at = (lane_code[:, :1] == code_row).astype(f32).astype(bf16)
    place[...] = jnp.dot(listed_at, hit, preferred_element_type=f32).astype(bf16)
    n = lax.shift_right_logical(slot_code, 7)
    m = n * own - (lax.bitwise_and(slot_code, 127) - K_MAX) * other
    m = jnp.where(n > 0, m, 0)
    wave = lax.bitwise_and(m + PITCH // 2, PITCH - 1) - PITCH // 2
    sigma = OMEGA * n.astype(f32) * own.astype(f32)
    kappa = KAPPA * wave.astype(f32) / PITCH
    lane = iota((1, LANES), 1)
    sign = jnp.where(lane < SLOT_LANES, -1.0, 1.0)
    terms[...] = jnp.zeros(terms.shape, f32)
    terms[0:1] = sign * sigma
    terms[1:2] = sign * kappa
    terms[2:3] = RELAX / (4.0 + sigma * sigma)


def transform_kernel(cells, tables, *rest):
    out, weights, arrived = rest[-3:]
    mine = lax.axis_index("row")
    fetches = [
        pltpu.make_async_copy(tables.at[mine, part], weights.at[part], arrived.at[part])
        for part in range(2)
    ]
    for fetch in fetches:
        fetch.start()
    lane = iota((8, LANES), 1)
    sub = iota((8, LANES), 0)
    parts = []
    for half in range(2):
        x = [cells[2 * p + half] for p in range(N_PITCH)]
        z = [x[p] + x[p + 16] for p in range(16)]
        even = [None] + [z[p] + z[16 - p] for p in range(1, 8)]
        odd = [None] + [z[p] - z[16 - p] for p in range(1, 8)]
        columns = []
        for t in range(9):
            re = z[0] + z[8] if t % 2 == 0 else z[0] - z[8]
            im = jnp.zeros((8, LANES), f32)
            for p in range(1, 8):
                re = re + math.cos(2.0 * math.pi * ((t * p) % 16) / 16) * even[p]
                if t % 8:
                    im = im - math.sin(2.0 * math.pi * ((t * p) % 16) / 16) * odd[p]

            def edge(value, offset):
                spread = jnp.broadcast_to(value[5:6, :], (8, LANES))
                return jnp.sum(jnp.where(lane == sub + offset, spread, 0.0), axis=1, keepdims=True)

            cos, sin = math.cos(2.0 * math.pi * t / 16), math.sin(2.0 * math.pi * t / 16)
            low_re, high_re = edge(re, 0), edge(re, 8)
            low_im, high_im = (edge(im, 0), edge(im, 8)) if t % 8 else (0.0, 0.0)
            re = re + jnp.where(lane == LANES - 1, cos * low_re - sin * low_im, 0.0)
            re = re + jnp.where(lane == 0, cos * high_re + sin * high_im, 0.0)
            im = im + jnp.where(lane == LANES - 1, cos * low_im + sin * low_re, 0.0)
            im = im + jnp.where(lane == 0, cos * high_im - sin * high_re, 0.0)
            columns += [re, im]
        parts.append(columns)
    for fetch in fetches:
        fetch.wait()
    wide = iota((16, LANES), 1)
    spot = lax.bitwise_and(wide, SLOT_LANES - 1)
    side = jnp.where(spot < HALF_CLASS, 1.0, -1.0)
    for group in range(GROUPS):
        re_lanes = jnp.zeros((16, LANES), f32)
        im_lanes = jnp.zeros((16, LANES), f32)
        for member in range(3):
            t = group * 3 + member
            left = jnp.concatenate(
                [parts[0][2 * t], parts[1][2 * t], parts[0][2 * t + 1], parts[1][2 * t + 1]], axis=0
            )
            high = left.astype(bf16)
            low = (left - high.astype(f32)).astype(bf16)
            both = jnp.dot(
                jnp.concatenate([high, low], axis=0), weights[0, t], preferred_element_type=f32
            )
            value = both[:32] + both[32:]
            value = value + jnp.dot(high, weights[1, t], preferred_element_type=f32)
            of_re, of_im = value[:16], pltpu.roll(value[16:], SLOT_LANES, 1)
            re = jnp.where(wide < SLOT_LANES, of_re, -of_re) + side * of_im
            im = pltpu.roll(re, SLOT_LANES, 1)
            first = member * CLASS_LANES
            if first:
                re, im = pltpu.roll(re, first, 1), pltpu.roll(im, first, 1)
            own = (wide >= first) & (wide < first + CLASS_LANES)
            re_lanes = jnp.where(own, re, re_lanes)
            im_lanes = jnp.where(own, im, im_lanes)
        out[0:16, group * LANES : (group + 1) * LANES] = re_lanes
        out[16:32, group * LANES : (group + 1) * LANES] = im_lanes


def place_kernel(values, place, out):
    x = values[...]
    high = x.astype(bf16)
    low = (x - high.astype(f32)).astype(bf16)
    split = jnp.concatenate([high, low], axis=0)
    lane = iota((8, LANES), 1)
    for block in range(N_PITCH // 4):
        picked = jnp.dot(
            split, place[:, 2 * block * LANES : 2 * (block + 1) * LANES], preferred_element_type=f32
        )
        picked = picked[0:32] + picked[32:64]
        for pair in range(2):
            here = picked[:, pair * LANES : (pair + 1) * LANES]
            at = 8 * block + 4 * pair
            for half in range(2):
                re, im = here[half * 8 : half * 8 + 8], here[16 + half * 8 : 24 + half * 8]
                out[at + half] = jnp.where(lane < SLOT_LANES, re, pltpu.roll(im, SLOT_LANES, 1))
                out[at + 2 + half] = jnp.where(lane < SLOT_LANES, pltpu.roll(re, SLOT_LANES, 1), im)


SPAN = RAD + 8


def turned(value):
    return pltpu.roll(value, SLOT_LANES, 1)


def swept(start, inside, jac, terms):
    length = start[0].shape[0]
    sigma, kappa, scale = terms[0:1], terms[1:2], terms[2:3]
    start = [w * inside for w in start]
    current = start
    for _ in range(2):
        above = [pltpu.roll(w, length - 1, 0) for w in current]
        below = [pltpu.roll(w, 1, 0) for w in current]
        grade = [above[f] - below[f] for f in range(F)]
        update = []
        for g in range(F):
            w = current[g]
            applied = 2.0 * w - 0.5 * (above[g] + below[g]) + sigma * turned(w)
            applied = applied + kappa * turned(mix(sweep_row(jac, 0, g), current))
            applied = applied + 0.5 * mix(sweep_row(jac, 1, g), grade)
            rest = start[g] - applied
            update.append((w + scale * (2.0 * rest - sigma * turned(rest))) * inside)
        current = update
    return current


def domain(radius):
    rad = lax.axis_index("rad")
    outside = ((radius < 0) & (rad == 0)) | ((radius >= RAD) & (rad == N_RAD - 1))
    return jnp.where(outside, 0.0, 1.0)


def beyond(modes, f):
    index = iota((8, LANES), 0)
    before = jnp.where(index == 7, modes[f, 6:7, :], 0.0)
    after = jnp.where(index == 0, modes[F + f, 6:7, :], 0.0)
    return before, after


def edge_kernel(jac, modes, terms, after, near, far):
    index = iota((32, LANES), 0)
    inside = domain(jnp.where(index < 16, index - 8, index + RAD - 24))
    start = []
    for f in range(F):
        low, high = beyond(modes, f)
        start.append(jnp.concatenate([low, modes[0:8, f, :], modes[RAD - 8 :, f, :], high], axis=0))
    rad_even = lax.rem(lax.axis_index("rad"), 2) == 0
    for f, w in enumerate(swept(start, inside, jac, terms)):
        near[f] = jnp.where(rad_even, w[24:], w[:8])
        far[f] = jnp.where(rad_even, w[:8], w[24:])


def sweep_kernel(jac, modes, terms, main):
    inside = domain(iota((RAD + 16, LANES), 0) - 8)
    start = []
    for f in range(F):
        low, high = beyond(modes, f)
        start.append(jnp.concatenate([low, modes[:, f, :], high], axis=0))
    for f, w in enumerate(swept(start, inside, jac, terms)):
        main[f] = w[8 : 8 + RAD]


def finish_kernel(main, near, far, out):
    index = iota((8, LANES), 0)
    rad_even = lax.rem(lax.axis_index("rad"), 2) == 0
    for f in range(F):
        from_low = jnp.where(rad_even, far[f], near[f])
        from_high = jnp.where(rad_even, near[f], far[f])
        first = main[f, 0:8] + jnp.where(index < 3, from_low, 0.0)
        last = main[f, RAD - 8 :] + jnp.where(index > 4, from_high, 0.0)
        body = jnp.concatenate([first, main[f, 8 : RAD - 8], last], axis=0)
        turned = jnp.transpose(body)
        out[pl.ds(2 * f, CAPACITY, 2 * F), :] = turned[:CAPACITY]
        out[pl.ds(2 * f + 1, CAPACITY, 2 * F), :] = turned[SLOT_LANES : SLOT_LANES + CAPACITY]


def shape(*dims, dtype=f32):
    return jax.ShapeDtypeStruct(dims, dtype)


def cost(flops, size):
    return pl.CostEstimate(flops=flops, bytes_accessed=size, transcendentals=0)


BIG = pltpu.CompilerParams(vmem_limit_bytes=20 * 1024 * 1024)


ANY = pl.BlockSpec(memory_space=pl.ANY)


def swap_pairs(count, first, periodic):
    pairs = []
    for i in range(first, count, 2):
        other = (i + 1) % count
        if other > i or periodic:
            pairs += [(i, other), (other, i)]
    return pairs


def on_device(flow, inflow, flux_jacobian, sweep_jacobian, mode_index, destination):
    weights, codes = fourier_tables()
    flux_jac = jnp.transpose(flux_jacobian, (1, 2, 0, 3))
    sweep_jac = jnp.transpose(sweep_jacobian, (0, 2, 1, 3))
    near_pitch, far_pitch = swap_pairs(N_PITCH, 0, True), swap_pairs(N_PITCH, 1, True)
    near_rad, far_rad = swap_pairs(N_RAD, 0, False), swap_pairs(N_RAD, 1, False)

    pinned = pltpu.with_memory_space_constraint(flow, pltpu.HBM)

    face = pl.pallas_call(
        exit_kernel,
        out_shape=shape(RAD, 8, LANES),
        in_specs=[ANY, ANY],
        out_specs=VMEM,
        scratch_shapes=[
            pltpu.VMEM((F, 2, RAD, LANES), f32),
            pltpu.SMEM((3, F, 1, F), f32),
            pltpu.SemaphoreType.DMA((F + 1,)),
        ],
        compiler_params=BIG,
        cost_estimate=cost(4_000_000, 600_000),
    )(pltpu.with_memory_space_constraint(flux_jac, pltpu.HBM), pinned)
    cells = lax.all_to_all(face, "pitch", 0, 0, tiled=True)

    faces = pl.pallas_call(
        halo_kernel,
        out_shape=(shape(RAD, LANES), shape(RAD, LANES), shape(F, AXIAL, LANES), shape(F, AXIAL, LANES)),
        in_specs=[VMEM],
        out_specs=(VMEM,) * 4,
        compiler_params=BIG,
        cost_estimate=cost(4_000_000, 1_400_000),
    )(flow)
    pitch_near = lax.ppermute(faces[0], "pitch", near_pitch)
    pitch_far = lax.ppermute(faces[1], "pitch", far_pitch)
    place, terms = pl.pallas_call(
        table_kernel,
        out_shape=(shape(TABLE, PACKED, dtype=bf16), shape(8, LANES)),
        in_specs=[VMEM, VMEM, VMEM],
        out_specs=(VMEM,) * 2,
        compiler_params=BIG,
        cost_estimate=cost(2 * TABLE * MODES * PACKED, 2_000_000),
    )(jnp.swapaxes(destination, 1, 2), mode_index, codes)

    modes = pl.pallas_call(
        transform_kernel,
        out_shape=shape(32, TABLE),
        in_specs=[VMEM, ANY, ANY, ANY, ANY],
        out_specs=VMEM,
        scratch_shapes=[
            pltpu.VMEM((2, 9, LANES, LANES), bf16),
            pltpu.SemaphoreType.DMA((2,)),
        ],
        compiler_params=BIG,
        cost_estimate=cost(60_000_000, 3_000_000),
    )(
        cells,
        pltpu.with_memory_space_constraint(jnp.asarray(weights), pltpu.HBM),
        place,
        pitch_near,
        pitch_far,
    )
    modes = lax.ppermute(modes, "row", [(0, 1), (1, 0)])
    placed = pl.pallas_call(
        place_kernel,
        out_shape=shape(RAD, 8, LANES),
        in_specs=[VMEM, VMEM],
        out_specs=VMEM,
        compiler_params=BIG,
        cost_estimate=cost(150_000_000, 2_000_000),
    )(modes, place)
    amplitude = lax.all_to_all(placed, "pitch", 0, 0, tiled=True)

    rows = lax.optimization_barrier((faces[2], faces[3], placed))[:2]
    rad_near = lax.ppermute(rows[0], "rad", near_rad)
    rad_far = lax.ppermute(rows[1], "rad", far_rad)
    next_flow, flux_done = pl.pallas_call(
        flux_kernel,
        grid=(AXIAL // DEPTH,),
        out_shape=(shape(1, F, AXIAL, RAD, LANES), shape(8, LANES)),
        in_specs=[
            SMEM,
            pl.BlockSpec((1, F, DEPTH, RAD, LANES), lambda z: (0, 0, z, 0, 0)),
            pl.BlockSpec((1, F, RAD, LANES), lambda z: (0, 0, 0, 0)),
            pl.BlockSpec((RAD, LANES), lambda z: (0, 0)),
            pl.BlockSpec((RAD, LANES), lambda z: (0, 0)),
            pl.BlockSpec((F, AXIAL, LANES), lambda z: (0, 0, 0)),
            pl.BlockSpec((F, AXIAL, LANES), lambda z: (0, 0, 0)),
            ANY,
        ],
        out_specs=(
            pl.BlockSpec((1, F, DEPTH, RAD, LANES), lambda z: (0, 0, z, 0, 0)),
            pl.BlockSpec((8, LANES), lambda z: (0, 0)),
        ),
        scratch_shapes=[pltpu.VMEM((F, RAD, LANES), f32)],
        compiler_params=BIG,
        cost_estimate=cost(20_000_000, 3_000_000),
    )(flux_jac, flow, inflow, pitch_near, pitch_far, rad_near, rad_far, placed)

    near, far = pl.pallas_call(
        edge_kernel,
        out_shape=(shape(F, 8, LANES), shape(F, 8, LANES)),
        in_specs=[SMEM, VMEM, VMEM, ANY],
        out_specs=(VMEM,) * 2,
        compiler_params=BIG,
        cost_estimate=cost(2_000_000, 300_000),
    )(sweep_jac, amplitude, terms, flux_done)
    near = lax.ppermute(near, "rad", near_rad)
    far = lax.ppermute(far, "rad", far_rad)
    main = pl.pallas_call(
        sweep_kernel,
        out_shape=shape(F, RAD, LANES),
        in_specs=[SMEM, VMEM, VMEM],
        out_specs=VMEM,
        compiler_params=BIG,
        cost_estimate=cost(8_000_000, 500_000),
    )(sweep_jac, amplitude, terms)
    response = pl.pallas_call(
        finish_kernel,
        out_shape=shape(CAPACITY * F * 2, RAD),
        in_specs=[VMEM] * 3,
        out_specs=VMEM,
        compiler_params=BIG,
        cost_estimate=cost(1_000_000, 800_000),
    )(main, near, far)
    response = response.reshape(1, 1, CAPACITY, F, 2, RAD)
    return next_flow, jnp.swapaxes(response, 3, 4)


def solution(mesh):
    placed = (
        P("row", None, None, "rad", "pitch"),
        P("row", None, "rad", "pitch"),
        P("row", None, None, None),
        P("row", None, None, None),
        P(),
        P(),
    )
    return jax.shard_map(
        on_device,
        mesh=mesh,
        in_specs=placed,
        out_specs=(
            P("row", None, None, "rad", "pitch"),
            P("row", "pitch", None, None, None, "rad"),
        ),
        check_vma=False,
    )
```

```python
import math

import jax
import jax.numpy as jnp
import ml_dtypes
import numpy as np
from jax import lax
from jax.experimental import pallas as pl
from jax.experimental.pallas import tpu as pltpu
from jax.sharding import PartitionSpec as P

F = 5
BLADES = 22
VANES = 54
AXIAL = 8
HARMONICS = 4
MODES_PER = 128
MODES = 512
PITCH = 4096
K_MAX = 32
CAPACITY = 48
N_PITCH = 32
N_RAD = 4
RAD = 64
LANES = 128
GROUPS = 3
TABLE = GROUPS * LANES
SLOT_LANES = 64
PACKED = N_PITCH * SLOT_LANES

FLUX_PITCH = 0.25
FLUX_RAD = 0.25
FLUX_AXIAL = 0.5
FLUX_DIFFUSE = 0.1
RELAX = 0.7
OMEGA = 0.05
KAPPA = 2.0

f32 = jnp.float32
bf16 = jnp.bfloat16
SMEM = pl.BlockSpec(memory_space=pltpu.SMEM)
VMEM = pl.BlockSpec(memory_space=pltpu.VMEM)


def iota(shape, dim):
    return lax.broadcasted_iota(jnp.int32, shape, dim)


CLASS_LANES = 43
HALF_CLASS = 22


def fourier_tables():
    weights = np.zeros((2, 2, 9, LANES, LANES), np.float64)
    codes = np.full((2, 8, TABLE), -1, np.int32)
    j = np.arange(LANES)
    for b, (own, other) in enumerate(((BLADES, VANES), (VANES, BLADES))):
        used = np.zeros((9, 2), int)
        for n in range(1, HARMONICS + 1):
            for k in range(-K_MAX, K_MAX + 1):
                q = (n * own - k * other) // 2
                t = q % 16
                part, side = (t, 0) if t <= 8 else (16 - t, 1)
                lane = side * HALF_CLASS + used[part, side]
                used[part, side] += 1
                angle = 2.0 * np.pi * ((q * j) % 2048) / 2048.0
                weights[b, 0, part, :, lane] = np.cos(angle) / 64.0
                weights[b, 0, part, :, SLOT_LANES + lane] = np.sin(angle) / 64.0
                group, member = divmod(part, 3)
                codes[b, :, group * LANES + member * CLASS_LANES + lane] = n * 128 + k + K_MAX
        assert used.max() <= HALF_CLASS - 1
    high = weights[:, 0].astype(ml_dtypes.bfloat16)
    low = (weights[:, 0] - high.astype(np.float64)).astype(ml_dtypes.bfloat16)
    return np.stack([high, low], axis=1), codes


def mix(coefficients, parts):
    total = coefficients[0] * parts[0]
    for f in range(1, F):
        total = total + coefficients[f] * parts[f]
    return total


def flux_row(jac, k, g):
    return [jac[k, g, 0, f] for f in range(F)]


def sweep_row(jac, k, g):
    return [jac[0, g, k, f] for f in range(F)]


def exit_kernel(jacobian, flow, out, planes, jac, arrived):
    copies = [
        pltpu.make_async_copy(flow.at[0, f, pl.ds(AXIAL - 2, 2)], planes.at[f], arrived.at[f])
        for f in range(F)
    ]
    copies.append(pltpu.make_async_copy(jacobian, jac, arrived.at[F]))
    for copy in copies:
        copy.start()
    for copy in copies:
        copy.wait()
    now = [planes[f, 1] for f in range(F)]
    behind = [planes[f, 0] for f in range(F)]
    lane = iota((RAD, LANES), 1)
    row = iota((RAD, LANES), 0)
    change = [now[f] - behind[f] for f in range(F)]
    edges = jnp.zeros((RAD, LANES), f32)
    out[...] = jnp.zeros(out.shape, f32)
    for g in range(F):
        pitch = mix([FLUX_PITCH * c for c in flux_row(jac, 0, g)], now)
        radial = mix([FLUX_RAD * c for c in flux_row(jac, 1, g)], now)
        soft = FLUX_DIFFUSE * now[g]
        to_low, to_high = soft - pitch, soft + pitch
        inward, outward = soft - radial, soft + radial
        value = now[g] - mix([FLUX_AXIAL * c for c in flux_row(jac, 2, g)], change) - 4.0 * soft
        value = value + jnp.where(lane == LANES - 1, 0.0, pltpu.roll(to_low, LANES - 1, 1))
        value = value + jnp.where(lane == 0, 0.0, pltpu.roll(to_high, 1, 1))
        value = value + jnp.where(row == RAD - 1, 0.0, pltpu.roll(inward, RAD - 1, 0))
        value = value + jnp.where(row == 0, 0.0, pltpu.roll(outward, 1, 0))
        out[:, g, :] = value
        edges = jnp.where(lane == g, pltpu.roll(to_low, g, 1) if g else to_low, edges)
        edges = jnp.where(lane == 8 + g, pltpu.roll(to_high, 9 + g, 1), edges)
        out[g, 6:7, :] = inward[0:1]
        out[F + g, 6:7, :] = outward[RAD - 1 : RAD]
    out[:, 5, :] = edges


def halo_kernel(flow, pitch_near, pitch_far, rad_near, rad_far):
    lane = iota((RAD, LANES), 1)
    low = jnp.zeros((RAD, LANES), f32)
    high = jnp.zeros((RAD, LANES), f32)
    pitch_even = lax.rem(lax.axis_index("pitch"), 2) == 0
    rad_even = lax.rem(lax.axis_index("rad"), 2) == 0
    for f in range(F):
        for z in range(AXIAL):
            k = f * AXIAL + z
            block = flow[0, f, z]
            low = jnp.where(lane == k, pltpu.roll(block, k, 1) if k else block, low)
            high = jnp.where(lane == k, pltpu.roll(block, k + 1, 1), high)
            first, last = block[0:1], block[RAD - 1 : RAD]
            rad_near[f, z : z + 1, :] = jnp.where(rad_even, last, first)
            rad_far[f, z : z + 1, :] = jnp.where(rad_even, first, last)
    pitch_near[...] = jnp.where(pitch_even, high, low)
    pitch_far[...] = jnp.where(pitch_even, low, high)


DEPTH = 4
ROWS = 16


def flux_kernel(jac, flow, inflow, pitch_near, pitch_far, rad_near, rad_far, after, out, done, previous):
    step = pl.program_id(0)
    lane = iota((ROWS, LANES), 1)
    row = iota((ROWS, LANES), 0)
    pitch_even = lax.rem(lax.axis_index("pitch"), 2) == 0
    rad_even = lax.rem(lax.axis_index("rad"), 2) == 0

    @pl.when(step == 0)
    def _():
        previous[...] = inflow[0]

    pitch_jac = [[FLUX_PITCH * c for c in flux_row(jac, 0, g)] for g in range(F)]
    rad_jac = [[FLUX_RAD * c for c in flux_row(jac, 1, g)] for g in range(F)]
    axial_jac = [[FLUX_AXIAL * c for c in flux_row(jac, 2, g)] for g in range(F)]
    for z in range(DEPTH):
        axial = step * DEPTH + z
        for start in range(0, RAD, ROWS):
            rows = slice(start, start + ROWS)
            near, far = pitch_near[rows], pitch_far[rows]
            next_column = jnp.where(pitch_even, near, far)
            last_column = jnp.where(pitch_even, far, near)
            now, pitch, radial, change, total = [], [], [], [], []
            for f in range(F):
                block = flow[0, f, z, rows]
                k = f * AXIAL + axial
                right = pltpu.roll(next_column, LANES - 1 - k, 1)
                left = pltpu.roll(last_column, lax.bitwise_and(LANES - k, LANES - 1), 1)
                right = jnp.where(lane == LANES - 1, right, pltpu.roll(block, LANES - 1, 1))
                left = jnp.where(lane == 0, left, pltpu.roll(block, 1, 1))
                if start + ROWS < RAD:
                    above = flow[0, f, z, start + 1 : start + ROWS + 1]
                else:
                    edge_near, edge_far = rad_near[f, pl.ds(axial, 1), :], rad_far[f, pl.ds(axial, 1), :]
                    edge = jnp.where(rad_even, edge_near, edge_far)
                    above = jnp.where(row == ROWS - 1, edge, pltpu.roll(block, ROWS - 1, 0))
                if start:
                    below = flow[0, f, z, start - 1 : start + ROWS - 1]
                else:
                    edge_near, edge_far = rad_near[f, pl.ds(axial, 1), :], rad_far[f, pl.ds(axial, 1), :]
                    edge = jnp.where(rad_even, edge_far, edge_near)
                    below = jnp.where(row == 0, edge, pltpu.roll(block, 1, 0))
                behind = flow[0, f, z - 1, rows] if z else previous[f, rows]
                now.append(block)
                pitch.append(right - left)
                radial.append(above - below)
                change.append(block - behind)
                total.append((right + left) + (above + below))
            for g in range(F):
                flux = mix(pitch_jac[g], pitch) + mix(rad_jac[g], radial) + mix(axial_jac[g], change)
                soft = (1.0 - 4.0 * FLUX_DIFFUSE) * now[g] + FLUX_DIFFUSE * total[g]
                out[0, g, z, rows] = soft - flux
    for f in range(F):
        previous[f] = flow[0, f, DEPTH - 1]
    done[...] = jnp.zeros(done.shape, f32)


def table_kernel(dest, modes, codes, place, terms):
    source = lax.axis_index("row")
    own = jnp.where(source == 0, BLADES, VANES)
    other = jnp.where(source == 0, VANES, BLADES)
    dest_row = dest[source]
    listed = modes[source]
    code_row = jnp.concatenate(
        [listed[h : h + 1] + (K_MAX + 128 * (h + 1)) for h in range(HARMONICS)], axis=1
    )

    def column(row, block):
        part = row[:, block * LANES : (block + 1) * LANES]
        return jnp.transpose(jnp.broadcast_to(part, (LANES, LANES)))

    here = iota((LANES, LANES), 0)
    there = iota((LANES, LANES), 1)
    spread = iota((LANES, PACKED), 1)
    target = lax.axis_index("pitch") * SLOT_LANES + lax.bitwise_and(there, SLOT_LANES - 1)
    slot_code = jnp.zeros((1, LANES), jnp.int32)
    hits = []
    for block in range(MODES // LANES):
        dest_col = column(dest_row, block)
        before = jnp.zeros((LANES, LANES), f32)
        for past in range(block + 1):
            same = dest_col == dest_row[:, past * LANES : (past + 1) * LANES]
            if past == block:
                same = same & (there < here)
            before = before + same.astype(f32)
        rank = jnp.sum(before, axis=1, keepdims=True).astype(jnp.int32)
        slot = dest_col * SLOT_LANES + rank
        hits.append((slot[:, :1] == spread).astype(f32).astype(bf16))
        mine = jnp.where(slot == target, column(code_row, block), 0)
        slot_code = slot_code + jnp.sum(mine, axis=0, keepdims=True)
    hit = jnp.concatenate(hits, axis=0)
    code_table = codes[source]
    lane_code = jnp.concatenate([column(code_table[0:1], g) for g in range(GROUPS)], axis=0)
    listed_at = (lane_code[:, :1] == code_row).astype(f32).astype(bf16)
    place[...] = jnp.dot(listed_at, hit, preferred_element_type=f32).astype(bf16)
    n = lax.shift_right_logical(slot_code, 7)
    m = n * own - (lax.bitwise_and(slot_code, 127) - K_MAX) * other
    m = jnp.where(n > 0, m, 0)
    wave = lax.bitwise_and(m + PITCH // 2, PITCH - 1) - PITCH // 2
    sigma = OMEGA * n.astype(f32) * own.astype(f32)
    kappa = KAPPA * wave.astype(f32) / PITCH
    lane = iota((1, LANES), 1)
    sign = jnp.where(lane < SLOT_LANES, -1.0, 1.0)
    terms[...] = jnp.zeros(terms.shape, f32)
    terms[0:1] = sign * sigma
    terms[1:2] = sign * kappa
    terms[2:3] = RELAX / (4.0 + sigma * sigma)


def spectrum_kernel(cells, tables, place, *rest):
    out, values, weights, arrived = rest[-4:]
    mine = lax.axis_index("row")
    fetches = [
        pltpu.make_async_copy(tables.at[mine, part], weights.at[part], arrived.at[part])
        for part in range(2)
    ]
    for fetch in fetches:
        fetch.start()
    lane = iota((8, LANES), 1)
    sub = iota((8, LANES), 0)
    parts = []
    for half in range(2):
        x = [cells[2 * p + half] for p in range(N_PITCH)]
        z = [x[p] + x[p + 16] for p in range(16)]
        even = [None] + [z[p] + z[16 - p] for p in range(1, 8)]
        odd = [None] + [z[p] - z[16 - p] for p in range(1, 8)]
        columns = []
        for t in range(9):
            re = z[0] + z[8] if t % 2 == 0 else z[0] - z[8]
            im = jnp.zeros((8, LANES), f32)
            for p in range(1, 8):
                re = re + math.cos(2.0 * math.pi * ((t * p) % 16) / 16) * even[p]
                if t % 8:
                    im = im - math.sin(2.0 * math.pi * ((t * p) % 16) / 16) * odd[p]

            def edge(value, offset):
                spread = jnp.broadcast_to(value[5:6, :], (8, LANES))
                return jnp.sum(jnp.where(lane == sub + offset, spread, 0.0), axis=1, keepdims=True)

            cos, sin = math.cos(2.0 * math.pi * t / 16), math.sin(2.0 * math.pi * t / 16)
            low_re, high_re = edge(re, 0), edge(re, 8)
            low_im, high_im = (edge(im, 0), edge(im, 8)) if t % 8 else (0.0, 0.0)
            re = re + jnp.where(lane == LANES - 1, cos * low_re - sin * low_im, 0.0)
            re = re + jnp.where(lane == 0, cos * high_re + sin * high_im, 0.0)
            im = im + jnp.where(lane == LANES - 1, cos * low_im + sin * low_re, 0.0)
            im = im + jnp.where(lane == 0, cos * high_im - sin * high_re, 0.0)
            columns += [re, im]
        parts.append(columns)
    for fetch in fetches:
        fetch.wait()
    wide = iota((16, LANES), 1)
    spot = lax.bitwise_and(wide, SLOT_LANES - 1)
    side = jnp.where(spot < HALF_CLASS, 1.0, -1.0)
    for group in range(GROUPS):
        re_lanes = jnp.zeros((16, LANES), f32)
        im_lanes = jnp.zeros((16, LANES), f32)
        for member in range(3):
            t = group * 3 + member
            left = jnp.concatenate(
                [parts[0][2 * t], parts[1][2 * t], parts[0][2 * t + 1], parts[1][2 * t + 1]], axis=0
            )
            high = left.astype(bf16)
            low = (left - high.astype(f32)).astype(bf16)
            both = jnp.dot(
                jnp.concatenate([high, low], axis=0), weights[0, t], preferred_element_type=f32
            )
            value = both[:32] + both[32:]
            value = value + jnp.dot(high, weights[1, t], preferred_element_type=f32)
            of_re, of_im = value[:16], pltpu.roll(value[16:], SLOT_LANES, 1)
            re = jnp.where(wide < SLOT_LANES, of_re, -of_re) + side * of_im
            im = pltpu.roll(re, SLOT_LANES, 1)
            first = member * CLASS_LANES
            if first:
                re, im = pltpu.roll(re, first, 1), pltpu.roll(im, first, 1)
            own = (wide >= first) & (wide < first + CLASS_LANES)
            re_lanes = jnp.where(own, re, re_lanes)
            im_lanes = jnp.where(own, im, im_lanes)
        values[0:16, group * LANES : (group + 1) * LANES] = re_lanes
        values[16:32, group * LANES : (group + 1) * LANES] = im_lanes
    x = values[...]
    high = x.astype(bf16)
    low = (x - high.astype(f32)).astype(bf16)
    split = jnp.concatenate([high, low], axis=0)
    lane = iota((8, LANES), 1)
    for block in range(N_PITCH // 4):
        picked = jnp.dot(
            split, place[:, 2 * block * LANES : 2 * (block + 1) * LANES], preferred_element_type=f32
        )
        picked = picked[0:32] + picked[32:64]
        for pair in range(2):
            here = picked[:, pair * LANES : (pair + 1) * LANES]
            at = 8 * block + 4 * pair
            for half in range(2):
                re, im = here[half * 8 : half * 8 + 8], here[16 + half * 8 : 24 + half * 8]
                out[at + half] = jnp.where(lane < SLOT_LANES, re, pltpu.roll(im, SLOT_LANES, 1))
                out[at + 2 + half] = jnp.where(lane < SLOT_LANES, pltpu.roll(re, SLOT_LANES, 1), im)


SPAN = RAD + 8


def turned(value):
    return pltpu.roll(value, SLOT_LANES, 1)


def swept(start, inside, jac, terms):
    length = start[0].shape[0]
    sigma, kappa, scale = terms[0:1], terms[1:2], terms[2:3]
    start = [w * inside for w in start]
    current = start
    for _ in range(2):
        above = [pltpu.roll(w, length - 1, 0) for w in current]
        below = [pltpu.roll(w, 1, 0) for w in current]
        grade = [above[f] - below[f] for f in range(F)]
        update = []
        for g in range(F):
            w = current[g]
            applied = 2.0 * w - 0.5 * (above[g] + below[g]) + sigma * turned(w)
            applied = applied + kappa * turned(mix(sweep_row(jac, 0, g), current))
            applied = applied + 0.5 * mix(sweep_row(jac, 1, g), grade)
            rest = start[g] - applied
            update.append((w + scale * (2.0 * rest - sigma * turned(rest))) * inside)
        current = update
    return current


def domain(radius):
    rad = lax.axis_index("rad")
    outside = ((radius < 0) & (rad == 0)) | ((radius >= RAD) & (rad == N_RAD - 1))
    return jnp.where(outside, 0.0, 1.0)


def beyond(modes, f):
    index = iota((8, LANES), 0)
    before = jnp.where(index == 7, modes[f, 6:7, :], 0.0)
    after = jnp.where(index == 0, modes[F + f, 6:7, :], 0.0)
    return before, after


def sweep_kernel(jac, modes, terms, after, main, near, far):
    inside = domain(iota((RAD + 16, LANES), 0) - 8)
    rad_even = lax.rem(lax.axis_index("rad"), 2) == 0
    start = []
    for f in range(F):
        low, high = beyond(modes, f)
        start.append(jnp.concatenate([low, modes[:, f, :], high], axis=0))
    for f, w in enumerate(swept(start, inside, jac, terms)):
        main[f] = w[8 : 8 + RAD]
        near[f] = jnp.where(rad_even, w[8 + RAD :], w[:8])
        far[f] = jnp.where(rad_even, w[:8], w[8 + RAD :])


def finish_kernel(main, near, far, out):
    index = iota((8, LANES), 0)
    rad_even = lax.rem(lax.axis_index("rad"), 2) == 0
    for f in range(F):
        from_low = jnp.where(rad_even, far[f], near[f])
        from_high = jnp.where(rad_even, near[f], far[f])
        first = main[f, 0:8] + jnp.where(index < 3, from_low, 0.0)
        last = main[f, RAD - 8 :] + jnp.where(index > 4, from_high, 0.0)
        body = jnp.concatenate([first, main[f, 8 : RAD - 8], last], axis=0)
        turned = jnp.transpose(body)
        out[pl.ds(2 * f, CAPACITY, 2 * F), :] = turned[:CAPACITY]
        out[pl.ds(2 * f + 1, CAPACITY, 2 * F), :] = turned[SLOT_LANES : SLOT_LANES + CAPACITY]


def shape(*dims, dtype=f32):
    return jax.ShapeDtypeStruct(dims, dtype)


def cost(flops, size):
    return pl.CostEstimate(flops=flops, bytes_accessed=size, transcendentals=0)


BIG = pltpu.CompilerParams(vmem_limit_bytes=20 * 1024 * 1024)


ANY = pl.BlockSpec(memory_space=pl.ANY)


def swap_pairs(count, first, periodic):
    pairs = []
    for i in range(first, count, 2):
        other = (i + 1) % count
        if other > i or periodic:
            pairs += [(i, other), (other, i)]
    return pairs


def across(pairs):
    return [(row * N_RAD + i, (1 - row) * N_RAD + j) for row in range(2) for i, j in pairs]


def on_device(flow, inflow, flux_jacobian, sweep_jacobian, mode_index, destination):
    weights, codes = fourier_tables()
    flux_jac = jnp.transpose(flux_jacobian, (1, 2, 0, 3))
    near_pitch, far_pitch = swap_pairs(N_PITCH, 0, True), swap_pairs(N_PITCH, 1, True)
    near_rad, far_rad = swap_pairs(N_RAD, 0, False), swap_pairs(N_RAD, 1, False)

    pinned = pltpu.with_memory_space_constraint(flow, pltpu.HBM)

    face = pl.pallas_call(
        exit_kernel,
        out_shape=shape(RAD, 8, LANES),
        in_specs=[ANY, ANY],
        out_specs=VMEM,
        scratch_shapes=[
            pltpu.VMEM((F, 2, RAD, LANES), f32),
            pltpu.SMEM((3, F, 1, F), f32),
            pltpu.SemaphoreType.DMA((F + 1,)),
        ],
        compiler_params=BIG,
        cost_estimate=cost(4_000_000, 600_000),
    )(pltpu.with_memory_space_constraint(flux_jac, pltpu.HBM), pinned)
    cells = lax.all_to_all(face, "pitch", 0, 0, tiled=True)

    faces = pl.pallas_call(
        halo_kernel,
        out_shape=(shape(RAD, LANES), shape(RAD, LANES), shape(F, AXIAL, LANES), shape(F, AXIAL, LANES)),
        in_specs=[VMEM],
        out_specs=(VMEM,) * 4,
        compiler_params=BIG,
        cost_estimate=cost(4_000_000, 1_400_000),
    )(flow)
    sweep_jac = jnp.transpose(sweep_jacobian, (0, 2, 1, 3))
    sweep_jac = lax.optimization_barrier((sweep_jac, faces[0]))[0]
    sweep_jac = lax.ppermute(sweep_jac, "row", [(0, 1), (1, 0)])
    pitch_near = lax.ppermute(faces[0], "pitch", near_pitch)
    pitch_far = lax.ppermute(faces[1], "pitch", far_pitch)
    place, terms = pl.pallas_call(
        table_kernel,
        out_shape=(shape(TABLE, PACKED, dtype=bf16), shape(8, LANES)),
        in_specs=[VMEM, VMEM, VMEM],
        out_specs=(VMEM,) * 2,
        compiler_params=BIG,
        cost_estimate=cost(2 * TABLE * MODES * PACKED, 2_000_000),
    )(jnp.swapaxes(destination, 1, 2), mode_index, codes)

    placed = pl.pallas_call(
        spectrum_kernel,
        out_shape=shape(RAD, 8, LANES),
        in_specs=[VMEM, ANY, VMEM, ANY, ANY, ANY],
        out_specs=VMEM,
        scratch_shapes=[
            pltpu.VMEM((32, TABLE), f32),
            pltpu.VMEM((2, 9, LANES, LANES), bf16),
            pltpu.SemaphoreType.DMA((2,)),
        ],
        compiler_params=BIG,
        cost_estimate=cost(200_000_000, 3_000_000),
    )(
        cells,
        pltpu.with_memory_space_constraint(jnp.asarray(weights), pltpu.HBM),
        place,
        pitch_near,
        pitch_far,
        sweep_jac,
    )
    amplitude = lax.all_to_all(placed, "pitch", 0, 0, tiled=True)

    rows = lax.optimization_barrier((faces[2], faces[3], placed))[:2]
    rad_near = lax.ppermute(rows[0], "rad", near_rad)
    rad_far = lax.ppermute(rows[1], "rad", far_rad)
    next_flow, flux_done = pl.pallas_call(
        flux_kernel,
        grid=(AXIAL // DEPTH,),
        out_shape=(shape(1, F, AXIAL, RAD, LANES), shape(8, LANES)),
        in_specs=[
            SMEM,
            pl.BlockSpec((1, F, DEPTH, RAD, LANES), lambda z: (0, 0, z, 0, 0)),
            pl.BlockSpec((1, F, RAD, LANES), lambda z: (0, 0, 0, 0)),
            pl.BlockSpec((RAD, LANES), lambda z: (0, 0)),
            pl.BlockSpec((RAD, LANES), lambda z: (0, 0)),
            pl.BlockSpec((F, AXIAL, LANES), lambda z: (0, 0, 0)),
            pl.BlockSpec((F, AXIAL, LANES), lambda z: (0, 0, 0)),
            ANY,
        ],
        out_specs=(
            pl.BlockSpec((1, F, DEPTH, RAD, LANES), lambda z: (0, 0, z, 0, 0)),
            pl.BlockSpec((8, LANES), lambda z: (0, 0)),
        ),
        scratch_shapes=[pltpu.VMEM((F, RAD, LANES), f32)],
        compiler_params=BIG,
        cost_estimate=cost(20_000_000, 3_000_000),
    )(flux_jac, flow, inflow, pitch_near, pitch_far, rad_near, rad_far, placed)

    main, near, far = pl.pallas_call(
        sweep_kernel,
        out_shape=(shape(F, RAD, LANES), shape(F, 8, LANES), shape(F, 8, LANES)),
        in_specs=[SMEM, VMEM, VMEM, ANY],
        out_specs=(VMEM,) * 3,
        compiler_params=BIG,
        cost_estimate=cost(8_000_000, 500_000),
    )(sweep_jac, amplitude, terms, flux_done)
    near = lax.ppermute(near, ("row", "rad"), across(near_rad))
    far = lax.ppermute(far, ("row", "rad"), across(far_rad))
    main = lax.ppermute(main, "row", [(0, 1), (1, 0)])
    response = pl.pallas_call(
        finish_kernel,
        out_shape=shape(CAPACITY * F * 2, RAD),
        in_specs=[VMEM] * 3,
        out_specs=VMEM,
        compiler_params=BIG,
        cost_estimate=cost(1_000_000, 800_000),
    )(main, near, far)
    response = response.reshape(1, 1, CAPACITY, F, 2, RAD)
    return next_flow, jnp.swapaxes(response, 3, 4)


def solution(mesh):
    placed = (
        P("row", None, None, "rad", "pitch"),
        P("row", None, "rad", "pitch"),
        P("row", None, None, None),
        P("row", None, None, None),
        P(),
        P(),
    )
    return jax.shard_map(
        on_device,
        mesh=mesh,
        in_specs=placed,
        out_specs=(
            P("row", None, None, "rad", "pitch"),
            P("row", "pitch", None, None, None, "rad"),
        ),
        check_vma=False,
    )
```

```python
import math

import jax
import jax.numpy as jnp
import ml_dtypes
import numpy as np
from jax import lax
from jax.experimental import pallas as pl
from jax.experimental.pallas import tpu as pltpu
from jax.sharding import PartitionSpec as P

F = 5
BLADES = 22
VANES = 54
AXIAL = 8
HARMONICS = 4
MODES_PER = 128
MODES = 512
PITCH = 4096
K_MAX = 32
CAPACITY = 48
N_PITCH = 32
N_RAD = 4
RAD = 64
LANES = 128
GROUPS = 3
TABLE = GROUPS * LANES
SLOT_LANES = 64
PACKED = N_PITCH * SLOT_LANES
ROWS_EACH = 12
SENT = N_PITCH * ROWS_EACH

FLUX_PITCH = 0.25
FLUX_RAD = 0.25
FLUX_AXIAL = 0.5
FLUX_DIFFUSE = 0.1
RELAX = 0.7
OMEGA = 0.05
KAPPA = 2.0

f32 = jnp.float32
bf16 = jnp.bfloat16
SMEM = pl.BlockSpec(memory_space=pltpu.SMEM)
VMEM = pl.BlockSpec(memory_space=pltpu.VMEM)


def iota(shape, dim):
    return lax.broadcasted_iota(jnp.int32, shape, dim)


CLASS_LANES = 43
HALF_CLASS = 22


def fourier_tables():
    weights = np.zeros((2, 2, 9, LANES, LANES), np.float64)
    codes = np.full((2, 8, TABLE), -1, np.int32)
    j = np.arange(LANES)
    for b, (own, other) in enumerate(((BLADES, VANES), (VANES, BLADES))):
        used = np.zeros((9, 2), int)
        for n in range(1, HARMONICS + 1):
            for k in range(-K_MAX, K_MAX + 1):
                q = (n * own - k * other) // 2
                t = q % 16
                part, side = (t, 0) if t <= 8 else (16 - t, 1)
                lane = side * HALF_CLASS + used[part, side]
                used[part, side] += 1
                angle = 2.0 * np.pi * ((q * j) % 2048) / 2048.0
                weights[b, 0, part, :, lane] = np.cos(angle) / 64.0
                weights[b, 0, part, :, SLOT_LANES + lane] = np.sin(angle) / 64.0
                group, member = divmod(part, 3)
                codes[b, :, group * LANES + member * CLASS_LANES + lane] = n * 128 + k + K_MAX
        assert used.max() <= HALF_CLASS - 1
    high = weights[:, 0].astype(ml_dtypes.bfloat16)
    low = (weights[:, 0] - high.astype(np.float64)).astype(ml_dtypes.bfloat16)
    return np.stack([high, low], axis=1), codes


def mix(coefficients, parts):
    total = coefficients[0] * parts[0]
    for f in range(1, F):
        total = total + coefficients[f] * parts[f]
    return total


def flux_row(jac, k, g):
    return [jac[k, g, 0, f] for f in range(F)]


def sweep_row(jac, k, g):
    return [jac[0, g, k, f] for f in range(F)]


def exit_kernel(jacobian, flow, out, planes, jac, fields, edges, arrived):
    copies = [
        pltpu.make_async_copy(flow.at[0, f, pl.ds(AXIAL - 2, 2)], planes.at[f], arrived.at[f])
        for f in range(F)
    ]
    copies.append(pltpu.make_async_copy(jacobian, jac, arrived.at[F]))
    for copy in copies:
        copy.start()
    for copy in copies:
        copy.wait()
    now = [planes[f, 1] for f in range(F)]
    behind = [planes[f, 0] for f in range(F)]
    lane = iota((RAD, LANES), 1)
    row = iota((RAD, LANES), 0)
    change = [now[f] - behind[f] for f in range(F)]
    edge = jnp.zeros((RAD, LANES), f32)
    out[pl.ds(11, N_PITCH, ROWS_EACH), :] = jnp.zeros((N_PITCH, LANES), f32)
    for g in range(F):
        pitch = mix([FLUX_PITCH * c for c in flux_row(jac, 0, g)], now)
        radial = mix([FLUX_RAD * c for c in flux_row(jac, 1, g)], now)
        soft = FLUX_DIFFUSE * now[g]
        to_low, to_high = soft - pitch, soft + pitch
        inward, outward = soft - radial, soft + radial
        value = now[g] - mix([FLUX_AXIAL * c for c in flux_row(jac, 2, g)], change) - 4.0 * soft
        value = value + jnp.where(lane == LANES - 1, 0.0, pltpu.roll(to_low, LANES - 1, 1))
        value = value + jnp.where(lane == 0, 0.0, pltpu.roll(to_high, 1, 1))
        value = value + jnp.where(row == RAD - 1, 0.0, pltpu.roll(inward, RAD - 1, 0))
        value = value + jnp.where(row == 0, 0.0, pltpu.roll(outward, 1, 0))
        fields[g] = value
        edge = jnp.where(lane == g, pltpu.roll(to_low, g, 1) if g else to_low, edge)
        edge = jnp.where(lane == 8 + g, pltpu.roll(to_high, 9 + g, 1), edge)
        for side in range(2):
            out[pl.ds(side * F + g, N_PITCH, ROWS_EACH), :] = fields[g, pl.ds(side, N_PITCH, 2), :]
        out[ROWS_EACH * g + 11 : ROWS_EACH * g + 12, :] = inward[0:1]
        out[ROWS_EACH * (F + g) + 11 : ROWS_EACH * (F + g) + 12, :] = outward[RAD - 1 : RAD]
    edges[...] = edge
    even, odd = edges[pl.ds(0, N_PITCH, 2), :], edges[pl.ds(1, N_PITCH, 2), :]
    lane = iota((N_PITCH, LANES), 1)
    both = jnp.where(lane < F, even, 0.0)
    both = jnp.where((lane >= F) & (lane < 2 * F), pltpu.roll(odd, F, 1), both)
    both = jnp.where((lane >= 16) & (lane < 16 + F), pltpu.roll(even, 8, 1), both)
    both = jnp.where((lane >= 16 + F) & (lane < 16 + 2 * F), pltpu.roll(odd, 8 + F, 1), both)
    out[pl.ds(10, N_PITCH, ROWS_EACH), :] = both


def halo_kernel(flow, pitch_near, pitch_far, rad_near, rad_far):
    lane = iota((RAD, LANES), 1)
    low = jnp.zeros((RAD, LANES), f32)
    high = jnp.zeros((RAD, LANES), f32)
    pitch_even = lax.rem(lax.axis_index("pitch"), 2) == 0
    rad_even = lax.rem(lax.axis_index("rad"), 2) == 0
    for f in range(F):
        for z in range(AXIAL):
            k = f * AXIAL + z
            block = flow[0, f, z]
            low = jnp.where(lane == k, pltpu.roll(block, k, 1) if k else block, low)
            high = jnp.where(lane == k, pltpu.roll(block, k + 1, 1), high)
            first, last = block[0:1], block[RAD - 1 : RAD]
            rad_near[f, z : z + 1, :] = jnp.where(rad_even, last, first)
            rad_far[f, z : z + 1, :] = jnp.where(rad_even, first, last)
    pitch_near[...] = jnp.where(pitch_even, high, low)
    pitch_far[...] = jnp.where(pitch_even, low, high)


DEPTH = 4
ROWS = 16


def flux_kernel(jac, flow, inflow, pitch_near, pitch_far, rad_near, rad_far, after, out, done, previous):
    step = pl.program_id(0)
    lane = iota((ROWS, LANES), 1)
    row = iota((ROWS, LANES), 0)
    pitch_even = lax.rem(lax.axis_index("pitch"), 2) == 0
    rad_even = lax.rem(lax.axis_index("rad"), 2) == 0

    @pl.when(step == 0)
    def _():
        previous[...] = inflow[0]

    pitch_jac = [[FLUX_PITCH * c for c in flux_row(jac, 0, g)] for g in range(F)]
    rad_jac = [[FLUX_RAD * c for c in flux_row(jac, 1, g)] for g in range(F)]
    axial_jac = [[FLUX_AXIAL * c for c in flux_row(jac, 2, g)] for g in range(F)]
    for z in range(DEPTH):
        axial = step * DEPTH + z
        for start in range(0, RAD, ROWS):
            rows = slice(start, start + ROWS)
            near, far = pitch_near[rows], pitch_far[rows]
            next_column = jnp.where(pitch_even, near, far)
            last_column = jnp.where(pitch_even, far, near)
            now, pitch, radial, change, total = [], [], [], [], []
            for f in range(F):
                block = flow[0, f, z, rows]
                k = f * AXIAL + axial
                right = pltpu.roll(next_column, LANES - 1 - k, 1)
                left = pltpu.roll(last_column, lax.bitwise_and(LANES - k, LANES - 1), 1)
                right = jnp.where(lane == LANES - 1, right, pltpu.roll(block, LANES - 1, 1))
                left = jnp.where(lane == 0, left, pltpu.roll(block, 1, 1))
                if start + ROWS < RAD:
                    above = flow[0, f, z, start + 1 : start + ROWS + 1]
                else:
                    edge_near, edge_far = rad_near[f, pl.ds(axial, 1), :], rad_far[f, pl.ds(axial, 1), :]
                    edge = jnp.where(rad_even, edge_near, edge_far)
                    above = jnp.where(row == ROWS - 1, edge, pltpu.roll(block, ROWS - 1, 0))
                if start:
                    below = flow[0, f, z, start - 1 : start + ROWS - 1]
                else:
                    edge_near, edge_far = rad_near[f, pl.ds(axial, 1), :], rad_far[f, pl.ds(axial, 1), :]
                    edge = jnp.where(rad_even, edge_far, edge_near)
                    below = jnp.where(row == 0, edge, pltpu.roll(block, 1, 0))
                behind = flow[0, f, z - 1, rows] if z else previous[f, rows]
                now.append(block)
                pitch.append(right - left)
                radial.append(above - below)
                change.append(block - behind)
                total.append((right + left) + (above + below))
            for g in range(F):
                flux = mix(pitch_jac[g], pitch) + mix(rad_jac[g], radial) + mix(axial_jac[g], change)
                soft = (1.0 - 4.0 * FLUX_DIFFUSE) * now[g] + FLUX_DIFFUSE * total[g]
                out[0, g, z, rows] = soft - flux
    for f in range(F):
        previous[f] = flow[0, f, DEPTH - 1]
    done[...] = jnp.zeros(done.shape, f32)


def table_kernel(dest, modes, codes, place, terms):
    source = lax.axis_index("row")
    own = jnp.where(source == 0, BLADES, VANES)
    other = jnp.where(source == 0, VANES, BLADES)
    dest_row = dest[source]
    listed = modes[source]
    code_row = jnp.concatenate(
        [listed[h : h + 1] + (K_MAX + 128 * (h + 1)) for h in range(HARMONICS)], axis=1
    )

    def column(row, block):
        part = row[:, block * LANES : (block + 1) * LANES]
        return jnp.transpose(jnp.broadcast_to(part, (LANES, LANES)))

    here = iota((LANES, LANES), 0)
    there = iota((LANES, LANES), 1)
    spread = iota((LANES, PACKED), 1)
    target = lax.axis_index("pitch") * SLOT_LANES + lax.bitwise_and(there, SLOT_LANES - 1)
    slot_code = jnp.zeros((1, LANES), jnp.int32)
    hits = []
    for block in range(MODES // LANES):
        dest_col = column(dest_row, block)
        before = jnp.zeros((LANES, LANES), f32)
        for past in range(block + 1):
            same = dest_col == dest_row[:, past * LANES : (past + 1) * LANES]
            if past == block:
                same = same & (there < here)
            before = before + same.astype(f32)
        rank = jnp.sum(before, axis=1, keepdims=True).astype(jnp.int32)
        slot = dest_col * SLOT_LANES + rank
        hits.append((slot[:, :1] == spread).astype(f32).astype(bf16))
        mine = jnp.where(slot == target, column(code_row, block), 0)
        slot_code = slot_code + jnp.sum(mine, axis=0, keepdims=True)
    hit = jnp.concatenate(hits, axis=0)
    code_table = codes[source]
    lane_code = jnp.concatenate([column(code_table[0:1], g) for g in range(GROUPS)], axis=0)
    listed_at = (lane_code[:, :1] == code_row).astype(f32).astype(bf16)
    place[...] = jnp.dot(listed_at, hit, preferred_element_type=f32).astype(bf16)
    n = lax.shift_right_logical(slot_code, 7)
    m = n * own - (lax.bitwise_and(slot_code, 127) - K_MAX) * other
    m = jnp.where(n > 0, m, 0)
    wave = lax.bitwise_and(m + PITCH // 2, PITCH - 1) - PITCH // 2
    sigma = OMEGA * n.astype(f32) * own.astype(f32)
    kappa = KAPPA * wave.astype(f32) / PITCH
    lane = iota((1, LANES), 1)
    sign = jnp.where(lane < SLOT_LANES, -1.0, 1.0)
    terms[...] = jnp.zeros(terms.shape, f32)
    terms[0:1] = sign * sigma
    terms[1:2] = sign * kappa
    terms[2:3] = RELAX / (4.0 + sigma * sigma)


def spectrum_kernel(cells, tables, place, *rest):
    out, values, weights, arrived = rest[-4:]
    mine = lax.axis_index("row")
    fetches = [
        pltpu.make_async_copy(tables.at[mine, part], weights.at[part], arrived.at[part])
        for part in range(2)
    ]
    for fetch in fetches:
        fetch.start()
    lane = iota((8, LANES), 1)
    sub = iota((8, LANES), 0)
    parts = []
    for half in range(2):
        first = [ROWS_EACH * p + 4 * half for p in range(N_PITCH)]
        x = [cells[at : at + 8] for at in first]
        z = [x[p] + x[p + 16] for p in range(16)]
        even = [None] + [z[p] + z[16 - p] for p in range(1, 8)]
        odd = [None] + [z[p] - z[16 - p] for p in range(1, 8)]
        columns = []
        for t in range(9):
            re = z[0] + z[8] if t % 2 == 0 else z[0] - z[8]
            im = jnp.zeros((8, LANES), f32)
            for p in range(1, 8):
                re = re + math.cos(2.0 * math.pi * ((t * p) % 16) / 16) * even[p]
                if t % 8:
                    im = im - math.sin(2.0 * math.pi * ((t * p) % 16) / 16) * odd[p]
            columns.append((re, im))
        parts.append(columns)

    def edge(value, half, offset):
        spread = jnp.broadcast_to(value[6:7, :], (8, LANES))
        own = lane == sub + (offset + 4 * half)
        return jnp.sum(jnp.where(own, spread, 0.0), axis=1, keepdims=True)

    closed = []
    for half in range(2):
        columns = []
        for t in range(9):
            re, im = parts[half][t]
            edge_re, edge_im = parts[1][t]
            cos, sin = math.cos(2.0 * math.pi * t / 16), math.sin(2.0 * math.pi * t / 16)
            low_re, high_re = edge(edge_re, half, 0), edge(edge_re, half, 16)
            low_im, high_im = 0.0, 0.0
            if t % 8:
                low_im, high_im = edge(edge_im, half, 0), edge(edge_im, half, 16)
            re = re + jnp.where(lane == LANES - 1, cos * low_re - sin * low_im, 0.0)
            re = re + jnp.where(lane == 0, cos * high_re + sin * high_im, 0.0)
            im = im + jnp.where(lane == LANES - 1, cos * low_im + sin * low_re, 0.0)
            im = im + jnp.where(lane == 0, cos * high_im - sin * high_re, 0.0)
            columns += [re, im]
        closed.append(columns)
    for fetch in fetches:
        fetch.wait()
    wide = iota((16, LANES), 1)
    spot = lax.bitwise_and(wide, SLOT_LANES - 1)
    side = jnp.where(spot < HALF_CLASS, 1.0, -1.0)
    for group in range(GROUPS):
        re_lanes = jnp.zeros((16, LANES), f32)
        im_lanes = jnp.zeros((16, LANES), f32)
        for member in range(3):
            t = group * 3 + member
            left = jnp.concatenate(
                [closed[0][2 * t], closed[1][2 * t], closed[0][2 * t + 1], closed[1][2 * t + 1]], axis=0
            )
            high = left.astype(bf16)
            low = (left - high.astype(f32)).astype(bf16)
            both = jnp.dot(
                jnp.concatenate([high, low], axis=0), weights[0, t], preferred_element_type=f32
            )
            value = both[:32] + both[32:]
            value = value + jnp.dot(high, weights[1, t], preferred_element_type=f32)
            of_re, of_im = value[:16], pltpu.roll(value[16:], SLOT_LANES, 1)
            re = jnp.where(wide < SLOT_LANES, of_re, -of_re) + side * of_im
            im = pltpu.roll(re, SLOT_LANES, 1)
            first = member * CLASS_LANES
            if first:
                re, im = pltpu.roll(re, first, 1), pltpu.roll(im, first, 1)
            own = (wide >= first) & (wide < first + CLASS_LANES)
            re_lanes = jnp.where(own, re, re_lanes)
            im_lanes = jnp.where(own, im, im_lanes)
        values[0:16, group * LANES : (group + 1) * LANES] = re_lanes
        values[16:32, group * LANES : (group + 1) * LANES] = im_lanes
    x = values[...]
    high = x.astype(bf16)
    low = (x - high.astype(f32)).astype(bf16)
    split = jnp.concatenate([high, low], axis=0)
    lane = iota((8, LANES), 1)
    for block in range(N_PITCH // 4):
        picked = jnp.dot(
            split, place[:, 2 * block * LANES : 2 * (block + 1) * LANES], preferred_element_type=f32
        )
        picked = picked[0:32] + picked[32:64]
        for pair in range(2):
            here = picked[:, pair * LANES : (pair + 1) * LANES]
            at = ROWS_EACH * (4 * block + 2 * pair)
            for half in range(2):
                re, im = here[half * 8 : half * 8 + 8], here[16 + half * 8 : 24 + half * 8]
                spot = at + 4 * half
                out[spot : spot + 8] = jnp.where(lane < SLOT_LANES, re, pltpu.roll(im, SLOT_LANES, 1))
                spot = spot + ROWS_EACH
                out[spot : spot + 8] = jnp.where(lane < SLOT_LANES, pltpu.roll(re, SLOT_LANES, 1), im)


SPAN = RAD + 8


def turned(value):
    return pltpu.roll(value, SLOT_LANES, 1)


def swept(start, inside, jac, terms):
    length = start[0].shape[0]
    sigma, kappa, scale = terms[0:1], terms[1:2], terms[2:3]
    start = [w * inside for w in start]
    current = start
    for _ in range(2):
        above = [pltpu.roll(w, length - 1, 0) for w in current]
        below = [pltpu.roll(w, 1, 0) for w in current]
        grade = [above[f] - below[f] for f in range(F)]
        update = []
        for g in range(F):
            w = current[g]
            applied = 2.0 * w - 0.5 * (above[g] + below[g]) + sigma * turned(w)
            applied = applied + kappa * turned(mix(sweep_row(jac, 0, g), current))
            applied = applied + 0.5 * mix(sweep_row(jac, 1, g), grade)
            rest = start[g] - applied
            update.append((w + scale * (2.0 * rest - sigma * turned(rest))) * inside)
        current = update
    return current


def domain(radius):
    rad = lax.axis_index("rad")
    outside = ((radius < 0) & (rad == 0)) | ((radius >= RAD) & (rad == N_RAD - 1))
    return jnp.where(outside, 0.0, 1.0)


def beyond(modes, f):
    index = iota((8, LANES), 0)
    at = [ROWS_EACH * d + 11 for d in (f, F + f)]
    before = jnp.where(index == 7, modes[at[0] : at[0] + 1], 0.0)
    after = jnp.where(index == 0, modes[at[1] : at[1] + 1], 0.0)
    return before, after


def sweep_kernel(jac, modes, terms, after, main, near, far, body):
    inside = domain(iota((RAD + 16, LANES), 0) - 8)
    rad_even = lax.rem(lax.axis_index("rad"), 2) == 0
    start = []
    for f in range(F):
        low, high = beyond(modes, f)
        for side in range(2):
            body[f, pl.ds(side, N_PITCH, 2), :] = modes[pl.ds(side * F + f, N_PITCH, ROWS_EACH), :]
        start.append(jnp.concatenate([low, body[f], high], axis=0))
    for f, w in enumerate(swept(start, inside, jac, terms)):
        main[f] = w[8 : 8 + RAD]
        near[f] = jnp.where(rad_even, w[8 + RAD :], w[:8])
        far[f] = jnp.where(rad_even, w[:8], w[8 + RAD :])


def finish_kernel(main, near, far, out):
    index = iota((8, LANES), 0)
    rad_even = lax.rem(lax.axis_index("rad"), 2) == 0
    for f in range(F):
        from_low = jnp.where(rad_even, far[f], near[f])
        from_high = jnp.where(rad_even, near[f], far[f])
        first = main[f, 0:8] + jnp.where(index < 3, from_low, 0.0)
        last = main[f, RAD - 8 :] + jnp.where(index > 4, from_high, 0.0)
        body = jnp.concatenate([first, main[f, 8 : RAD - 8], last], axis=0)
        turned = jnp.transpose(body)
        out[pl.ds(2 * f, CAPACITY, 2 * F), :] = turned[:CAPACITY]
        out[pl.ds(2 * f + 1, CAPACITY, 2 * F), :] = turned[SLOT_LANES : SLOT_LANES + CAPACITY]


def shape(*dims, dtype=f32):
    return jax.ShapeDtypeStruct(dims, dtype)


def cost(flops, size):
    return pl.CostEstimate(flops=flops, bytes_accessed=size, transcendentals=0)


BIG = pltpu.CompilerParams(vmem_limit_bytes=20 * 1024 * 1024)


ANY = pl.BlockSpec(memory_space=pl.ANY)


def swap_pairs(count, first, periodic):
    pairs = []
    for i in range(first, count, 2):
        other = (i + 1) % count
        if other > i or periodic:
            pairs += [(i, other), (other, i)]
    return pairs


def transposed(value):
    value = value.reshape(SENT // 4, 4, LANES)
    return lax.all_to_all(value, "pitch", 0, 0, tiled=True).reshape(SENT, LANES)


def across(pairs):
    return [(row * N_RAD + i, (1 - row) * N_RAD + j) for row in range(2) for i, j in pairs]


def on_device(flow, inflow, flux_jacobian, sweep_jacobian, mode_index, destination):
    weights, codes = fourier_tables()
    flux_jac = jnp.transpose(flux_jacobian, (1, 2, 0, 3))
    near_pitch, far_pitch = swap_pairs(N_PITCH, 0, True), swap_pairs(N_PITCH, 1, True)
    near_rad, far_rad = swap_pairs(N_RAD, 0, False), swap_pairs(N_RAD, 1, False)

    pinned = pltpu.with_memory_space_constraint(flow, pltpu.HBM)

    face = pl.pallas_call(
        exit_kernel,
        out_shape=shape(SENT, LANES),
        in_specs=[ANY, ANY],
        out_specs=VMEM,
        scratch_shapes=[
            pltpu.VMEM((F, 2, RAD, LANES), f32),
            pltpu.SMEM((3, F, 1, F), f32),
            pltpu.VMEM((F, RAD, LANES), f32),
            pltpu.VMEM((RAD, LANES), f32),
            pltpu.SemaphoreType.DMA((F + 1,)),
        ],
        compiler_params=BIG,
        cost_estimate=cost(4_000_000, 600_000),
    )(pltpu.with_memory_space_constraint(flux_jac, pltpu.HBM), pinned)
    cells = transposed(face)

    faces = pl.pallas_call(
        halo_kernel,
        out_shape=(shape(RAD, LANES), shape(RAD, LANES), shape(F, AXIAL, LANES), shape(F, AXIAL, LANES)),
        in_specs=[VMEM],
        out_specs=(VMEM,) * 4,
        compiler_params=BIG,
        cost_estimate=cost(4_000_000, 1_400_000),
    )(flow)
    sweep_jac = jnp.transpose(sweep_jacobian, (0, 2, 1, 3))
    sweep_jac = lax.optimization_barrier((sweep_jac, faces[0]))[0]
    sweep_jac = lax.ppermute(sweep_jac, "row", [(0, 1), (1, 0)])
    pitch_near = lax.ppermute(faces[0], "pitch", near_pitch)
    pitch_far = lax.ppermute(faces[1], "pitch", far_pitch)
    place, terms = pl.pallas_call(
        table_kernel,
        out_shape=(shape(TABLE, PACKED, dtype=bf16), shape(8, LANES)),
        in_specs=[VMEM, VMEM, VMEM],
        out_specs=(VMEM,) * 2,
        compiler_params=BIG,
        cost_estimate=cost(2 * TABLE * MODES * PACKED, 2_000_000),
    )(jnp.swapaxes(destination, 1, 2), mode_index, codes)

    placed = pl.pallas_call(
        spectrum_kernel,
        out_shape=shape(SENT, LANES),
        in_specs=[VMEM, ANY, VMEM, ANY, ANY, ANY],
        out_specs=VMEM,
        scratch_shapes=[
            pltpu.VMEM((32, TABLE), f32),
            pltpu.VMEM((2, 9, LANES, LANES), bf16),
            pltpu.SemaphoreType.DMA((2,)),
        ],
        compiler_params=BIG,
        cost_estimate=cost(200_000_000, 3_000_000),
    )(
        cells,
        pltpu.with_memory_space_constraint(jnp.asarray(weights), pltpu.HBM),
        place,
        pitch_near,
        pitch_far,
        sweep_jac,
    )
    amplitude = transposed(placed)

    rows = lax.optimization_barrier((faces[2], faces[3], placed))[:2]
    rad_near = lax.ppermute(rows[0], "rad", near_rad)
    rad_far = lax.ppermute(rows[1], "rad", far_rad)
    next_flow, flux_done = pl.pallas_call(
        flux_kernel,
        grid=(AXIAL // DEPTH,),
        out_shape=(shape(1, F, AXIAL, RAD, LANES), shape(8, LANES)),
        in_specs=[
            SMEM,
            pl.BlockSpec((1, F, DEPTH, RAD, LANES), lambda z: (0, 0, z, 0, 0)),
            pl.BlockSpec((1, F, RAD, LANES), lambda z: (0, 0, 0, 0)),
            pl.BlockSpec((RAD, LANES), lambda z: (0, 0)),
            pl.BlockSpec((RAD, LANES), lambda z: (0, 0)),
            pl.BlockSpec((F, AXIAL, LANES), lambda z: (0, 0, 0)),
            pl.BlockSpec((F, AXIAL, LANES), lambda z: (0, 0, 0)),
            ANY,
        ],
        out_specs=(
            pl.BlockSpec((1, F, DEPTH, RAD, LANES), lambda z: (0, 0, z, 0, 0)),
            pl.BlockSpec((8, LANES), lambda z: (0, 0)),
        ),
        scratch_shapes=[pltpu.VMEM((F, RAD, LANES), f32)],
        compiler_params=BIG,
        cost_estimate=cost(20_000_000, 3_000_000),
    )(flux_jac, flow, inflow, pitch_near, pitch_far, rad_near, rad_far, placed)

    main, near, far = pl.pallas_call(
        sweep_kernel,
        out_shape=(shape(F, RAD, LANES), shape(F, 8, LANES), shape(F, 8, LANES)),
        in_specs=[SMEM, VMEM, VMEM, ANY],
        out_specs=(VMEM,) * 3,
        scratch_shapes=[pltpu.VMEM((F, RAD, LANES), f32)],
        compiler_params=BIG,
        cost_estimate=cost(8_000_000, 500_000),
    )(sweep_jac, amplitude, terms, flux_done)
    near = lax.ppermute(near, ("row", "rad"), across(near_rad))
    far = lax.ppermute(far, ("row", "rad"), across(far_rad))
    main = lax.ppermute(main, "row", [(0, 1), (1, 0)])
    response = pl.pallas_call(
        finish_kernel,
        out_shape=shape(CAPACITY * F * 2, RAD),
        in_specs=[VMEM] * 3,
        out_specs=VMEM,
        compiler_params=BIG,
        cost_estimate=cost(1_000_000, 800_000),
    )(main, near, far)
    response = response.reshape(1, 1, CAPACITY, F, 2, RAD)
    return next_flow, jnp.swapaxes(response, 3, 4)


def solution(mesh):
    placed = (
        P("row", None, None, "rad", "pitch"),
        P("row", None, "rad", "pitch"),
        P("row", None, None, None),
        P("row", None, None, None),
        P(),
        P(),
    )
    return jax.shard_map(
        on_device,
        mesh=mesh,
        in_specs=placed,
        out_specs=(
            P("row", None, None, "rad", "pitch"),
            P("row", "pitch", None, None, None, "rad"),
        ),
        check_vma=False,
    )
```

```python
import math

import jax
import jax.numpy as jnp
import ml_dtypes
import numpy as np
from jax import lax
from jax.experimental import pallas as pl
from jax.experimental.pallas import tpu as pltpu
from jax.sharding import PartitionSpec as P

F = 5
BLADES = 22
VANES = 54
AXIAL = 8
HARMONICS = 4
MODES_PER = 128
MODES = 512
PITCH = 4096
K_MAX = 32
CAPACITY = 48
N_PITCH = 32
N_RAD = 4
RAD = 64
LANES = 128
GROUPS = 3
TABLE = GROUPS * LANES
SLOT_LANES = 64
PACKED = N_PITCH * SLOT_LANES
ROWS_EACH = 12
SENT = N_PITCH * ROWS_EACH

FLUX_PITCH = 0.25
FLUX_RAD = 0.25
FLUX_AXIAL = 0.5
FLUX_DIFFUSE = 0.1
RELAX = 0.7
OMEGA = 0.05
KAPPA = 2.0

f32 = jnp.float32
bf16 = jnp.bfloat16
SMEM = pl.BlockSpec(memory_space=pltpu.SMEM)
VMEM = pl.BlockSpec(memory_space=pltpu.VMEM)


def iota(shape, dim):
    return lax.broadcasted_iota(jnp.int32, shape, dim)


CLASS_LANES = 43
HALF_CLASS = 22


def fourier_tables():
    weights = np.zeros((2, 2, 9, LANES, LANES), np.float64)
    codes = np.full((2, 8, TABLE), -1, np.int32)
    j = np.arange(LANES)
    for b, (own, other) in enumerate(((BLADES, VANES), (VANES, BLADES))):
        used = np.zeros((9, 2), int)
        for n in range(1, HARMONICS + 1):
            for k in range(-K_MAX, K_MAX + 1):
                q = (n * own - k * other) // 2
                t = q % 16
                part, side = (t, 0) if t <= 8 else (16 - t, 1)
                lane = side * HALF_CLASS + used[part, side]
                used[part, side] += 1
                angle = 2.0 * np.pi * ((q * j) % 2048) / 2048.0
                weights[b, 0, part, :, lane] = np.cos(angle) / 64.0
                weights[b, 0, part, :, SLOT_LANES + lane] = np.sin(angle) / 64.0
                group, member = divmod(part, 3)
                codes[b, :, group * LANES + member * CLASS_LANES + lane] = n * 128 + k + K_MAX
        assert used.max() <= HALF_CLASS - 1
    high = weights[:, 0].astype(ml_dtypes.bfloat16)
    low = (weights[:, 0] - high.astype(np.float64)).astype(ml_dtypes.bfloat16)
    return np.stack([high, low], axis=1), codes


def mix(coefficients, parts):
    total = coefficients[0] * parts[0]
    for f in range(1, F):
        total = total + coefficients[f] * parts[f]
    return total


def flux_row(jac, k, g):
    return [jac[k, g, 0, f] for f in range(F)]


def sweep_row(jac, k, g):
    return [jac[0, g, k, f] for f in range(F)]


def exit_kernel(jacobian, flow, out, planes, jac, fields, edges, arrived):
    copies = [
        pltpu.make_async_copy(flow.at[0, f, pl.ds(AXIAL - 2, 2)], planes.at[f], arrived.at[f])
        for f in range(F)
    ]
    copies.append(pltpu.make_async_copy(jacobian, jac, arrived.at[F]))
    for copy in copies:
        copy.start()
    for copy in copies:
        copy.wait()
    now = [planes[f, 1] for f in range(F)]
    behind = [planes[f, 0] for f in range(F)]
    lane = iota((RAD, LANES), 1)
    row = iota((RAD, LANES), 0)
    change = [now[f] - behind[f] for f in range(F)]
    edge = jnp.zeros((RAD, LANES), f32)
    out[pl.ds(11, N_PITCH, ROWS_EACH), :] = jnp.zeros((N_PITCH, LANES), f32)
    for g in range(F):
        pitch = mix([FLUX_PITCH * c for c in flux_row(jac, 0, g)], now)
        radial = mix([FLUX_RAD * c for c in flux_row(jac, 1, g)], now)
        soft = FLUX_DIFFUSE * now[g]
        to_low, to_high = soft - pitch, soft + pitch
        inward, outward = soft - radial, soft + radial
        value = now[g] - mix([FLUX_AXIAL * c for c in flux_row(jac, 2, g)], change) - 4.0 * soft
        value = value + jnp.where(lane == LANES - 1, 0.0, pltpu.roll(to_low, LANES - 1, 1))
        value = value + jnp.where(lane == 0, 0.0, pltpu.roll(to_high, 1, 1))
        value = value + jnp.where(row == RAD - 1, 0.0, pltpu.roll(inward, RAD - 1, 0))
        value = value + jnp.where(row == 0, 0.0, pltpu.roll(outward, 1, 0))
        fields[g] = value
        edge = jnp.where(lane == g, pltpu.roll(to_low, g, 1) if g else to_low, edge)
        edge = jnp.where(lane == 8 + g, pltpu.roll(to_high, 9 + g, 1), edge)
        for side in range(2):
            out[pl.ds(side * F + g, N_PITCH, ROWS_EACH), :] = fields[g, pl.ds(side, N_PITCH, 2), :]
        out[ROWS_EACH * g + 11 : ROWS_EACH * g + 12, :] = inward[0:1]
        out[ROWS_EACH * (F + g) + 11 : ROWS_EACH * (F + g) + 12, :] = outward[RAD - 1 : RAD]
    edges[...] = edge
    even, odd = edges[pl.ds(0, N_PITCH, 2), :], edges[pl.ds(1, N_PITCH, 2), :]
    lane = iota((N_PITCH, LANES), 1)
    both = jnp.where(lane < F, even, 0.0)
    both = jnp.where((lane >= F) & (lane < 2 * F), pltpu.roll(odd, F, 1), both)
    both = jnp.where((lane >= 16) & (lane < 16 + F), pltpu.roll(even, 8, 1), both)
    both = jnp.where((lane >= 16 + F) & (lane < 16 + 2 * F), pltpu.roll(odd, 8 + F, 1), both)
    out[pl.ds(10, N_PITCH, ROWS_EACH), :] = both


def halo_kernel(flow, pitch_near, pitch_far, rad_near, rad_far):
    lane = iota((RAD, LANES), 1)
    low = jnp.zeros((RAD, LANES), f32)
    high = jnp.zeros((RAD, LANES), f32)
    pitch_even = lax.rem(lax.axis_index("pitch"), 2) == 0
    rad_even = lax.rem(lax.axis_index("rad"), 2) == 0
    for f in range(F):
        for z in range(AXIAL):
            k = f * AXIAL + z
            block = flow[0, f, z]
            low = jnp.where(lane == k, pltpu.roll(block, k, 1) if k else block, low)
            high = jnp.where(lane == k, pltpu.roll(block, k + 1, 1), high)
            first, last = block[0:1], block[RAD - 1 : RAD]
            rad_near[f, z : z + 1, :] = jnp.where(rad_even, last, first)
            rad_far[f, z : z + 1, :] = jnp.where(rad_even, first, last)
    pitch_near[...] = jnp.where(pitch_even, high, low)
    pitch_far[...] = jnp.where(pitch_even, low, high)


DEPTH = 4
ROWS = 16


def flux_kernel(jac, flow, inflow, pitch_near, pitch_far, rad_near, rad_far, after, out, done, previous):
    step = pl.program_id(0)
    lane = iota((ROWS, LANES), 1)
    row = iota((ROWS, LANES), 0)
    pitch_even = lax.rem(lax.axis_index("pitch"), 2) == 0
    rad_even = lax.rem(lax.axis_index("rad"), 2) == 0

    @pl.when(step == 0)
    def _():
        previous[...] = inflow[0]

    pitch_jac = [[FLUX_PITCH * c for c in flux_row(jac, 0, g)] for g in range(F)]
    rad_jac = [[FLUX_RAD * c for c in flux_row(jac, 1, g)] for g in range(F)]
    axial_jac = [[FLUX_AXIAL * c for c in flux_row(jac, 2, g)] for g in range(F)]
    for z in range(DEPTH):
        axial = step * DEPTH + z
        for start in range(0, RAD, ROWS):
            rows = slice(start, start + ROWS)
            near, far = pitch_near[rows], pitch_far[rows]
            next_column = jnp.where(pitch_even, near, far)
            last_column = jnp.where(pitch_even, far, near)
            now, pitch, radial, change, total = [], [], [], [], []
            for f in range(F):
                block = flow[0, f, z, rows]
                k = f * AXIAL + axial
                right = pltpu.roll(next_column, LANES - 1 - k, 1)
                left = pltpu.roll(last_column, lax.bitwise_and(LANES - k, LANES - 1), 1)
                right = jnp.where(lane == LANES - 1, right, pltpu.roll(block, LANES - 1, 1))
                left = jnp.where(lane == 0, left, pltpu.roll(block, 1, 1))
                if start + ROWS < RAD:
                    above = flow[0, f, z, start + 1 : start + ROWS + 1]
                else:
                    edge_near, edge_far = rad_near[f, pl.ds(axial, 1), :], rad_far[f, pl.ds(axial, 1), :]
                    edge = jnp.where(rad_even, edge_near, edge_far)
                    above = jnp.where(row == ROWS - 1, edge, pltpu.roll(block, ROWS - 1, 0))
                if start:
                    below = flow[0, f, z, start - 1 : start + ROWS - 1]
                else:
                    edge_near, edge_far = rad_near[f, pl.ds(axial, 1), :], rad_far[f, pl.ds(axial, 1), :]
                    edge = jnp.where(rad_even, edge_far, edge_near)
                    below = jnp.where(row == 0, edge, pltpu.roll(block, 1, 0))
                behind = flow[0, f, z - 1, rows] if z else previous[f, rows]
                now.append(block)
                pitch.append(right - left)
                radial.append(above - below)
                change.append(block - behind)
                total.append((right + left) + (above + below))
            for g in range(F):
                flux = mix(pitch_jac[g], pitch) + mix(rad_jac[g], radial) + mix(axial_jac[g], change)
                soft = (1.0 - 4.0 * FLUX_DIFFUSE) * now[g] + FLUX_DIFFUSE * total[g]
                out[0, g, z, rows] = soft - flux
    for f in range(F):
        previous[f] = flow[0, f, DEPTH - 1]
    done[...] = jnp.zeros(done.shape, f32)


def table_kernel(dest, modes, codes, tables, place, terms, weights, arrived):
    source = lax.axis_index("row")
    fetches = [
        pltpu.make_async_copy(tables.at[source, part], weights.at[part], arrived.at[part])
        for part in range(2)
    ]
    for fetch in fetches:
        fetch.start()
    own = jnp.where(source == 0, BLADES, VANES)
    other = jnp.where(source == 0, VANES, BLADES)
    dest_row = dest[source]
    listed = modes[source]
    code_row = jnp.concatenate(
        [listed[h : h + 1] + (K_MAX + 128 * (h + 1)) for h in range(HARMONICS)], axis=1
    )

    def column(row, block):
        part = row[:, block * LANES : (block + 1) * LANES]
        return jnp.transpose(jnp.broadcast_to(part, (LANES, LANES)))

    here = iota((LANES, LANES), 0)
    there = iota((LANES, LANES), 1)
    spread = iota((LANES, PACKED), 1)
    target = lax.axis_index("pitch") * SLOT_LANES + lax.bitwise_and(there, SLOT_LANES - 1)
    slot_code = jnp.zeros((1, LANES), jnp.int32)
    hits = []
    for block in range(MODES // LANES):
        dest_col = column(dest_row, block)
        before = jnp.zeros((LANES, LANES), f32)
        for past in range(block + 1):
            same = dest_col == dest_row[:, past * LANES : (past + 1) * LANES]
            if past == block:
                same = same & (there < here)
            before = before + same.astype(f32)
        rank = jnp.sum(before, axis=1, keepdims=True).astype(jnp.int32)
        slot = dest_col * SLOT_LANES + rank
        hits.append((slot[:, :1] == spread).astype(f32).astype(bf16))
        mine = jnp.where(slot == target, column(code_row, block), 0)
        slot_code = slot_code + jnp.sum(mine, axis=0, keepdims=True)
    hit = jnp.concatenate(hits, axis=0)
    code_table = codes[source]
    lane_code = jnp.concatenate([column(code_table[0:1], g) for g in range(GROUPS)], axis=0)
    listed_at = (lane_code[:, :1] == code_row).astype(f32).astype(bf16)
    place[...] = jnp.dot(listed_at, hit, preferred_element_type=f32).astype(bf16)
    n = lax.shift_right_logical(slot_code, 7)
    m = n * own - (lax.bitwise_and(slot_code, 127) - K_MAX) * other
    m = jnp.where(n > 0, m, 0)
    wave = lax.bitwise_and(m + PITCH // 2, PITCH - 1) - PITCH // 2
    sigma = OMEGA * n.astype(f32) * own.astype(f32)
    kappa = KAPPA * wave.astype(f32) / PITCH
    lane = iota((1, LANES), 1)
    sign = jnp.where(lane < SLOT_LANES, -1.0, 1.0)
    terms[...] = jnp.zeros(terms.shape, f32)
    terms[0:1] = sign * sigma
    terms[1:2] = sign * kappa
    terms[2:3] = RELAX / (4.0 + sigma * sigma)
    for fetch in fetches:
        fetch.wait()


def spectrum_kernel(cells, weights, place, *rest):
    out, values = rest[-2:]
    lane = iota((8, LANES), 1)
    sub = iota((8, LANES), 0)
    parts = []
    for half in range(2):
        first = [ROWS_EACH * p + 4 * half for p in range(N_PITCH)]
        x = [cells[at : at + 8] for at in first]
        z = [x[p] + x[p + 16] for p in range(16)]
        even = [None] + [z[p] + z[16 - p] for p in range(1, 8)]
        odd = [None] + [z[p] - z[16 - p] for p in range(1, 8)]
        columns = []
        for t in range(9):
            re = z[0] + z[8] if t % 2 == 0 else z[0] - z[8]
            im = jnp.zeros((8, LANES), f32)
            for p in range(1, 8):
                re = re + math.cos(2.0 * math.pi * ((t * p) % 16) / 16) * even[p]
                if t % 8:
                    im = im - math.sin(2.0 * math.pi * ((t * p) % 16) / 16) * odd[p]
            columns.append((re, im))
        parts.append(columns)

    def edge(value, half, offset):
        spread = jnp.broadcast_to(value[6:7, :], (8, LANES))
        own = lane == sub + (offset + 4 * half)
        return jnp.sum(jnp.where(own, spread, 0.0), axis=1, keepdims=True)

    closed = []
    for half in range(2):
        columns = []
        for t in range(9):
            re, im = parts[half][t]
            edge_re, edge_im = parts[1][t]
            cos, sin = math.cos(2.0 * math.pi * t / 16), math.sin(2.0 * math.pi * t / 16)
            low_re, high_re = edge(edge_re, half, 0), edge(edge_re, half, 16)
            low_im, high_im = 0.0, 0.0
            if t % 8:
                low_im, high_im = edge(edge_im, half, 0), edge(edge_im, half, 16)
            re = re + jnp.where(lane == LANES - 1, cos * low_re - sin * low_im, 0.0)
            re = re + jnp.where(lane == 0, cos * high_re + sin * high_im, 0.0)
            im = im + jnp.where(lane == LANES - 1, cos * low_im + sin * low_re, 0.0)
            im = im + jnp.where(lane == 0, cos * high_im - sin * high_re, 0.0)
            columns += [re, im]
        closed.append(columns)
    wide = iota((16, LANES), 1)
    spot = lax.bitwise_and(wide, SLOT_LANES - 1)
    side = jnp.where(spot < HALF_CLASS, 1.0, -1.0)
    for group in range(GROUPS):
        re_lanes = jnp.zeros((16, LANES), f32)
        im_lanes = jnp.zeros((16, LANES), f32)
        for member in range(3):
            t = group * 3 + member
            left = jnp.concatenate(
                [closed[0][2 * t], closed[1][2 * t], closed[0][2 * t + 1], closed[1][2 * t + 1]], axis=0
            )
            high = left.astype(bf16)
            low = (left - high.astype(f32)).astype(bf16)
            both = jnp.dot(
                jnp.concatenate([high, low], axis=0), weights[0, t], preferred_element_type=f32
            )
            value = both[:32] + both[32:]
            value = value + jnp.dot(high, weights[1, t], preferred_element_type=f32)
            of_re, of_im = value[:16], pltpu.roll(value[16:], SLOT_LANES, 1)
            re = jnp.where(wide < SLOT_LANES, of_re, -of_re) + side * of_im
            im = pltpu.roll(re, SLOT_LANES, 1)
            first = member * CLASS_LANES
            if first:
                re, im = pltpu.roll(re, first, 1), pltpu.roll(im, first, 1)
            own = (wide >= first) & (wide < first + CLASS_LANES)
            re_lanes = jnp.where(own, re, re_lanes)
            im_lanes = jnp.where(own, im, im_lanes)
        values[0:16, group * LANES : (group + 1) * LANES] = re_lanes
        values[16:32, group * LANES : (group + 1) * LANES] = im_lanes
    x = values[...]
    high = x.astype(bf16)
    low = (x - high.astype(f32)).astype(bf16)
    split = jnp.concatenate([high, low], axis=0)
    lane = iota((8, LANES), 1)
    for block in range(N_PITCH // 4):
        picked = jnp.dot(
            split, place[:, 2 * block * LANES : 2 * (block + 1) * LANES], preferred_element_type=f32
        )
        picked = picked[0:32] + picked[32:64]
        for pair in range(2):
            here = picked[:, pair * LANES : (pair + 1) * LANES]
            at = ROWS_EACH * (4 * block + 2 * pair)
            for half in range(2):
                re, im = here[half * 8 : half * 8 + 8], here[16 + half * 8 : 24 + half * 8]
                spot = at + 4 * half
                out[spot : spot + 8] = jnp.where(lane < SLOT_LANES, re, pltpu.roll(im, SLOT_LANES, 1))
                spot = spot + ROWS_EACH
                out[spot : spot + 8] = jnp.where(lane < SLOT_LANES, pltpu.roll(re, SLOT_LANES, 1), im)


SPAN = RAD + 8


def turned(value):
    return pltpu.roll(value, SLOT_LANES, 1)


def swept(start, inside, jac, terms):
    length = start[0].shape[0]
    sigma, kappa, scale = terms[0:1], terms[1:2], terms[2:3]
    start = [w * inside for w in start]
    current = start
    for _ in range(2):
        above = [pltpu.roll(w, length - 1, 0) for w in current]
        below = [pltpu.roll(w, 1, 0) for w in current]
        grade = [above[f] - below[f] for f in range(F)]
        update = []
        for g in range(F):
            w = current[g]
            applied = 2.0 * w - 0.5 * (above[g] + below[g]) + sigma * turned(w)
            applied = applied + kappa * turned(mix(sweep_row(jac, 0, g), current))
            applied = applied + 0.5 * mix(sweep_row(jac, 1, g), grade)
            rest = start[g] - applied
            update.append((w + scale * (2.0 * rest - sigma * turned(rest))) * inside)
        current = update
    return current


def domain(radius):
    rad = lax.axis_index("rad")
    outside = ((radius < 0) & (rad == 0)) | ((radius >= RAD) & (rad == N_RAD - 1))
    return jnp.where(outside, 0.0, 1.0)


def beyond(modes, f):
    index = iota((8, LANES), 0)
    at = [ROWS_EACH * d + 11 for d in (f, F + f)]
    before = jnp.where(index == 7, modes[at[0] : at[0] + 1], 0.0)
    after = jnp.where(index == 0, modes[at[1] : at[1] + 1], 0.0)
    return before, after


def sweep_kernel(jac, modes, terms, after, main, near, far, body):
    inside = domain(iota((RAD + 16, LANES), 0) - 8)
    rad_even = lax.rem(lax.axis_index("rad"), 2) == 0
    start = []
    for f in range(F):
        low, high = beyond(modes, f)
        for side in range(2):
            body[f, pl.ds(side, N_PITCH, 2), :] = modes[pl.ds(side * F + f, N_PITCH, ROWS_EACH), :]
        start.append(jnp.concatenate([low, body[f], high], axis=0))
    for f, w in enumerate(swept(start, inside, jac, terms)):
        main[f] = w[8 : 8 + RAD]
        near[f] = jnp.where(rad_even, w[8 + RAD :], w[:8])
        far[f] = jnp.where(rad_even, w[:8], w[8 + RAD :])


def finish_kernel(main, near, far, out):
    index = iota((8, LANES), 0)
    rad_even = lax.rem(lax.axis_index("rad"), 2) == 0
    for f in range(F):
        from_low = jnp.where(rad_even, far[f], near[f])
        from_high = jnp.where(rad_even, near[f], far[f])
        first = main[f, 0:8] + jnp.where(index < 3, from_low, 0.0)
        last = main[f, RAD - 8 :] + jnp.where(index > 4, from_high, 0.0)
        body = jnp.concatenate([first, main[f, 8 : RAD - 8], last], axis=0)
        turned = jnp.transpose(body)
        out[pl.ds(2 * f, CAPACITY, 2 * F), :] = turned[:CAPACITY]
        out[pl.ds(2 * f + 1, CAPACITY, 2 * F), :] = turned[SLOT_LANES : SLOT_LANES + CAPACITY]


def shape(*dims, dtype=f32):
    return jax.ShapeDtypeStruct(dims, dtype)


def cost(flops, size):
    return pl.CostEstimate(flops=flops, bytes_accessed=size, transcendentals=0)


BIG = pltpu.CompilerParams(vmem_limit_bytes=20 * 1024 * 1024)


ANY = pl.BlockSpec(memory_space=pl.ANY)


def swap_pairs(count, first, periodic):
    pairs = []
    for i in range(first, count, 2):
        other = (i + 1) % count
        if other > i or periodic:
            pairs += [(i, other), (other, i)]
    return pairs


def transposed(value):
    value = value.reshape(SENT // 4, 4, LANES)
    return lax.all_to_all(value, "pitch", 0, 0, tiled=True).reshape(SENT, LANES)


def across(pairs):
    return [(row * N_RAD + i, (1 - row) * N_RAD + j) for row in range(2) for i, j in pairs]


def on_device(flow, inflow, flux_jacobian, sweep_jacobian, mode_index, destination):
    weights, codes = fourier_tables()
    flux_jac = jnp.transpose(flux_jacobian, (1, 2, 0, 3))
    near_pitch, far_pitch = swap_pairs(N_PITCH, 0, True), swap_pairs(N_PITCH, 1, True)
    near_rad, far_rad = swap_pairs(N_RAD, 0, False), swap_pairs(N_RAD, 1, False)

    pinned = pltpu.with_memory_space_constraint(flow, pltpu.HBM)

    face = pl.pallas_call(
        exit_kernel,
        out_shape=shape(SENT, LANES),
        in_specs=[ANY, ANY],
        out_specs=VMEM,
        scratch_shapes=[
            pltpu.VMEM((F, 2, RAD, LANES), f32),
            pltpu.SMEM((3, F, 1, F), f32),
            pltpu.VMEM((F, RAD, LANES), f32),
            pltpu.VMEM((RAD, LANES), f32),
            pltpu.SemaphoreType.DMA((F + 1,)),
        ],
        compiler_params=BIG,
        cost_estimate=cost(4_000_000, 600_000),
    )(pltpu.with_memory_space_constraint(flux_jac, pltpu.HBM), pinned)
    cells = transposed(face)

    faces = pl.pallas_call(
        halo_kernel,
        out_shape=(shape(RAD, LANES), shape(RAD, LANES), shape(F, AXIAL, LANES), shape(F, AXIAL, LANES)),
        in_specs=[VMEM],
        out_specs=(VMEM,) * 4,
        compiler_params=BIG,
        cost_estimate=cost(4_000_000, 1_400_000),
    )(flow)
    pitch_near = lax.ppermute(faces[0], "pitch", near_pitch)
    pitch_far = lax.ppermute(faces[1], "pitch", far_pitch)
    place, terms, own_weights = pl.pallas_call(
        table_kernel,
        out_shape=(
            shape(TABLE, PACKED, dtype=bf16),
            shape(8, LANES),
            shape(2, 9, LANES, LANES, dtype=bf16),
        ),
        in_specs=[VMEM, VMEM, VMEM, ANY],
        out_specs=(VMEM,) * 3,
        scratch_shapes=[pltpu.SemaphoreType.DMA((2,))],
        compiler_params=BIG,
        cost_estimate=cost(2 * TABLE * MODES * PACKED, 2_000_000),
    )(
        jnp.swapaxes(destination, 1, 2),
        mode_index,
        codes,
        pltpu.with_memory_space_constraint(jnp.asarray(weights), pltpu.HBM),
    )

    placed = pl.pallas_call(
        spectrum_kernel,
        out_shape=shape(SENT, LANES),
        in_specs=[VMEM, VMEM, VMEM, ANY, ANY],
        out_specs=VMEM,
        scratch_shapes=[pltpu.VMEM((32, TABLE), f32)],
        compiler_params=BIG,
        cost_estimate=cost(200_000_000, 3_000_000),
    )(
        cells,
        own_weights,
        place,
        pitch_near,
        pitch_far,
    )
    amplitude = transposed(placed)

    sweep_jac = jnp.transpose(sweep_jacobian, (0, 2, 1, 3))
    *rows, sweep_jac = lax.optimization_barrier((faces[2], faces[3], sweep_jac, placed))[:3]
    sweep_jac = lax.ppermute(sweep_jac, "row", [(0, 1), (1, 0)])
    rad_near = lax.ppermute(rows[0], "rad", near_rad)
    rad_far = lax.ppermute(rows[1], "rad", far_rad)
    next_flow, flux_done = pl.pallas_call(
        flux_kernel,
        grid=(AXIAL // DEPTH,),
        out_shape=(shape(1, F, AXIAL, RAD, LANES), shape(8, LANES)),
        in_specs=[
            SMEM,
            pl.BlockSpec((1, F, DEPTH, RAD, LANES), lambda z: (0, 0, z, 0, 0)),
            pl.BlockSpec((1, F, RAD, LANES), lambda z: (0, 0, 0, 0)),
            pl.BlockSpec((RAD, LANES), lambda z: (0, 0)),
            pl.BlockSpec((RAD, LANES), lambda z: (0, 0)),
            pl.BlockSpec((F, AXIAL, LANES), lambda z: (0, 0, 0)),
            pl.BlockSpec((F, AXIAL, LANES), lambda z: (0, 0, 0)),
            ANY,
        ],
        out_specs=(
            pl.BlockSpec((1, F, DEPTH, RAD, LANES), lambda z: (0, 0, z, 0, 0)),
            pl.BlockSpec((8, LANES), lambda z: (0, 0)),
        ),
        scratch_shapes=[pltpu.VMEM((F, RAD, LANES), f32)],
        compiler_params=BIG,
        cost_estimate=cost(20_000_000, 3_000_000),
    )(flux_jac, pinned, inflow, pitch_near, pitch_far, rad_near, rad_far, placed)

    main, near, far = pl.pallas_call(
        sweep_kernel,
        out_shape=(shape(F, RAD, LANES), shape(F, 8, LANES), shape(F, 8, LANES)),
        in_specs=[SMEM, VMEM, VMEM, ANY],
        out_specs=(VMEM,) * 3,
        scratch_shapes=[pltpu.VMEM((F, RAD, LANES), f32)],
        compiler_params=BIG,
        cost_estimate=cost(8_000_000, 500_000),
    )(sweep_jac, amplitude, terms, flux_done)
    near = lax.ppermute(near, ("row", "rad"), across(near_rad))
    far = lax.ppermute(far, ("row", "rad"), across(far_rad))
    main = lax.ppermute(main, "row", [(0, 1), (1, 0)])
    response = pl.pallas_call(
        finish_kernel,
        out_shape=shape(CAPACITY * F * 2, RAD),
        in_specs=[VMEM] * 3,
        out_specs=VMEM,
        compiler_params=BIG,
        cost_estimate=cost(1_000_000, 800_000),
    )(main, near, far)
    response = response.reshape(1, 1, CAPACITY, F, 2, RAD)
    return next_flow, jnp.swapaxes(response, 3, 4)


def solution(mesh):
    placed = (
        P("row", None, None, "rad", "pitch"),
        P("row", None, "rad", "pitch"),
        P("row", None, None, None),
        P("row", None, None, None),
        P(),
        P(),
    )
    return jax.shard_map(
        on_device,
        mesh=mesh,
        in_specs=placed,
        out_specs=(
            P("row", None, None, "rad", "pitch"),
            P("row", "pitch", None, None, None, "rad"),
        ),
        check_vma=False,
    )
```

```python
import math

import jax
import jax.numpy as jnp
import ml_dtypes
import numpy as np
from jax import lax
from jax.experimental import pallas as pl
from jax.experimental.pallas import tpu as pltpu
from jax.sharding import PartitionSpec as P

F = 5
BLADES = 22
VANES = 54
AXIAL = 8
HARMONICS = 4
MODES_PER = 128
MODES = 512
PITCH = 4096
K_MAX = 32
CAPACITY = 48
N_PITCH = 32
N_RAD = 4
RAD = 64
LANES = 128
GROUPS = 3
TABLE = GROUPS * LANES
SLOT_LANES = 64
PACKED = N_PITCH * SLOT_LANES
ROWS_EACH = 12
SENT = N_PITCH * ROWS_EACH

FLUX_PITCH = 0.25
FLUX_RAD = 0.25
FLUX_AXIAL = 0.5
FLUX_DIFFUSE = 0.1
RELAX = 0.7
OMEGA = 0.05
KAPPA = 2.0

f32 = jnp.float32
bf16 = jnp.bfloat16
SMEM = pl.BlockSpec(memory_space=pltpu.SMEM)
VMEM = pl.BlockSpec(memory_space=pltpu.VMEM)


def iota(shape, dim):
    return lax.broadcasted_iota(jnp.int32, shape, dim)


CLASS_LANES = 43
HALF_CLASS = 22


def fourier_tables():
    weights = np.zeros((2, 2, 9, LANES, LANES), np.float64)
    codes = np.full((2, 8, TABLE), -1, np.int32)
    j = np.arange(LANES)
    for b, (own, other) in enumerate(((BLADES, VANES), (VANES, BLADES))):
        used = np.zeros((9, 2), int)
        for n in range(1, HARMONICS + 1):
            for k in range(-K_MAX, K_MAX + 1):
                q = (n * own - k * other) // 2
                t = q % 16
                part, side = (t, 0) if t <= 8 else (16 - t, 1)
                lane = side * HALF_CLASS + used[part, side]
                used[part, side] += 1
                angle = 2.0 * np.pi * ((q * j) % 2048) / 2048.0
                weights[b, 0, part, :, lane] = np.cos(angle) / 64.0
                weights[b, 0, part, :, SLOT_LANES + lane] = np.sin(angle) / 64.0
                group, member = divmod(part, 3)
                codes[b, :, group * LANES + member * CLASS_LANES + lane] = n * 128 + k + K_MAX
        assert used.max() <= HALF_CLASS - 1
    high = weights[:, 0].astype(ml_dtypes.bfloat16)
    low = (weights[:, 0] - high.astype(np.float64)).astype(ml_dtypes.bfloat16)
    return np.stack([high, low], axis=1), codes


def mix(coefficients, parts):
    total = coefficients[0] * parts[0]
    for f in range(1, F):
        total = total + coefficients[f] * parts[f]
    return total


def flux_row(jac, k, g):
    return [jac[k, g, 0, f] for f in range(F)]


def sweep_row(jac, k, g):
    return [jac[0, g, k, f] for f in range(F)]


def exit_kernel(jacobian, flow, out, planes, jac, fields, edges, arrived):
    copies = [
        pltpu.make_async_copy(flow.at[0, f, pl.ds(AXIAL - 2, 2)], planes.at[f], arrived.at[f])
        for f in range(F)
    ]
    copies.append(pltpu.make_async_copy(jacobian, jac, arrived.at[F]))
    for copy in copies:
        copy.start()
    for copy in copies:
        copy.wait()
    now = [planes[f, 1] for f in range(F)]
    behind = [planes[f, 0] for f in range(F)]
    lane = iota((RAD, LANES), 1)
    row = iota((RAD, LANES), 0)
    change = [now[f] - behind[f] for f in range(F)]
    edge = jnp.zeros((RAD, LANES), f32)
    out[pl.ds(11, N_PITCH, ROWS_EACH), :] = jnp.zeros((N_PITCH, LANES), f32)
    for g in range(F):
        pitch = mix([FLUX_PITCH * c for c in flux_row(jac, 0, g)], now)
        radial = mix([FLUX_RAD * c for c in flux_row(jac, 1, g)], now)
        soft = FLUX_DIFFUSE * now[g]
        to_low, to_high = soft - pitch, soft + pitch
        inward, outward = soft - radial, soft + radial
        value = now[g] - mix([FLUX_AXIAL * c for c in flux_row(jac, 2, g)], change) - 4.0 * soft
        value = value + jnp.where(lane == LANES - 1, 0.0, pltpu.roll(to_low, LANES - 1, 1))
        value = value + jnp.where(lane == 0, 0.0, pltpu.roll(to_high, 1, 1))
        value = value + jnp.where(row == RAD - 1, 0.0, pltpu.roll(inward, RAD - 1, 0))
        value = value + jnp.where(row == 0, 0.0, pltpu.roll(outward, 1, 0))
        fields[g] = value
        edge = jnp.where(lane == g, pltpu.roll(to_low, g, 1) if g else to_low, edge)
        edge = jnp.where(lane == 8 + g, pltpu.roll(to_high, 9 + g, 1), edge)
        for side in range(2):
            out[pl.ds(side * F + g, N_PITCH, ROWS_EACH), :] = fields[g, pl.ds(side, N_PITCH, 2), :]
        out[ROWS_EACH * g + 11 : ROWS_EACH * g + 12, :] = inward[0:1]
        out[ROWS_EACH * (F + g) + 11 : ROWS_EACH * (F + g) + 12, :] = outward[RAD - 1 : RAD]
    edges[...] = edge
    even, odd = edges[pl.ds(0, N_PITCH, 2), :], edges[pl.ds(1, N_PITCH, 2), :]
    lane = iota((N_PITCH, LANES), 1)
    both = jnp.where(lane < F, even, 0.0)
    both = jnp.where((lane >= F) & (lane < 2 * F), pltpu.roll(odd, F, 1), both)
    both = jnp.where((lane >= 16) & (lane < 16 + F), pltpu.roll(even, 8, 1), both)
    both = jnp.where((lane >= 16 + F) & (lane < 16 + 2 * F), pltpu.roll(odd, 8 + F, 1), both)
    out[pl.ds(10, N_PITCH, ROWS_EACH), :] = both


def halo_kernel(flow, pitch_near, pitch_far, rad_near, rad_far):
    lane = iota((RAD, LANES), 1)
    low = jnp.zeros((RAD, LANES), f32)
    high = jnp.zeros((RAD, LANES), f32)
    pitch_even = lax.rem(lax.axis_index("pitch"), 2) == 0
    rad_even = lax.rem(lax.axis_index("rad"), 2) == 0
    for f in range(F):
        for z in range(AXIAL):
            k = f * AXIAL + z
            block = flow[0, f, z]
            low = jnp.where(lane == k, pltpu.roll(block, k, 1) if k else block, low)
            high = jnp.where(lane == k, pltpu.roll(block, k + 1, 1), high)
            first, last = block[0:1], block[RAD - 1 : RAD]
            rad_near[f, z : z + 1, :] = jnp.where(rad_even, last, first)
            rad_far[f, z : z + 1, :] = jnp.where(rad_even, first, last)
    pitch_near[...] = jnp.where(pitch_even, high, low)
    pitch_far[...] = jnp.where(pitch_even, low, high)


DEPTH = 2
ROWS = 16


def flux_kernel(jac, flow, inflow, pitch_near, pitch_far, rad_near, rad_far, after, out, done, previous):
    step = pl.program_id(0)
    lane = iota((ROWS, LANES), 1)
    row = iota((ROWS, LANES), 0)
    pitch_even = lax.rem(lax.axis_index("pitch"), 2) == 0
    rad_even = lax.rem(lax.axis_index("rad"), 2) == 0

    @pl.when(step == 0)
    def _():
        previous[...] = inflow[0]

    pitch_jac = [[FLUX_PITCH * c for c in flux_row(jac, 0, g)] for g in range(F)]
    rad_jac = [[FLUX_RAD * c for c in flux_row(jac, 1, g)] for g in range(F)]
    axial_jac = [[FLUX_AXIAL * c for c in flux_row(jac, 2, g)] for g in range(F)]
    for z in range(DEPTH):
        axial = step * DEPTH + z
        for start in range(0, RAD, ROWS):
            rows = slice(start, start + ROWS)
            near, far = pitch_near[rows], pitch_far[rows]
            next_column = jnp.where(pitch_even, near, far)
            last_column = jnp.where(pitch_even, far, near)
            now, pitch, radial, change, total = [], [], [], [], []
            for f in range(F):
                block = flow[0, f, z, rows]
                k = f * AXIAL + axial
                right = pltpu.roll(next_column, LANES - 1 - k, 1)
                left = pltpu.roll(last_column, lax.bitwise_and(LANES - k, LANES - 1), 1)
                right = jnp.where(lane == LANES - 1, right, pltpu.roll(block, LANES - 1, 1))
                left = jnp.where(lane == 0, left, pltpu.roll(block, 1, 1))
                if start + ROWS < RAD:
                    above = flow[0, f, z, start + 1 : start + ROWS + 1]
                else:
                    edge_near, edge_far = rad_near[f, pl.ds(axial, 1), :], rad_far[f, pl.ds(axial, 1), :]
                    edge = jnp.where(rad_even, edge_near, edge_far)
                    above = jnp.where(row == ROWS - 1, edge, pltpu.roll(block, ROWS - 1, 0))
                if start:
                    below = flow[0, f, z, start - 1 : start + ROWS - 1]
                else:
                    edge_near, edge_far = rad_near[f, pl.ds(axial, 1), :], rad_far[f, pl.ds(axial, 1), :]
                    edge = jnp.where(rad_even, edge_far, edge_near)
                    below = jnp.where(row == 0, edge, pltpu.roll(block, 1, 0))
                behind = flow[0, f, z - 1, rows] if z else previous[f, rows]
                now.append(block)
                pitch.append(right - left)
                radial.append(above - below)
                change.append(block - behind)
                total.append((right + left) + (above + below))
            for g in range(F):
                flux = mix(pitch_jac[g], pitch) + mix(rad_jac[g], radial) + mix(axial_jac[g], change)
                soft = (1.0 - 4.0 * FLUX_DIFFUSE) * now[g] + FLUX_DIFFUSE * total[g]
                out[0, g, z, rows] = soft - flux
    for f in range(F):
        previous[f] = flow[0, f, DEPTH - 1]
    done[...] = jnp.zeros(done.shape, f32)


def table_kernel(dest, modes, codes, tables, place, terms, weights, arrived):
    source = lax.axis_index("row")
    fetches = [
        pltpu.make_async_copy(tables.at[source, part], weights.at[part], arrived.at[part])
        for part in range(2)
    ]
    for fetch in fetches:
        fetch.start()
    own = jnp.where(source == 0, BLADES, VANES)
    other = jnp.where(source == 0, VANES, BLADES)
    dest_row = dest[source]
    listed = modes[source]
    code_row = jnp.concatenate(
        [listed[h : h + 1] + (K_MAX + 128 * (h + 1)) for h in range(HARMONICS)], axis=1
    )

    def column(row, block):
        part = row[:, block * LANES : (block + 1) * LANES]
        return jnp.transpose(jnp.broadcast_to(part, (LANES, LANES)))

    here = iota((LANES, LANES), 0)
    there = iota((LANES, LANES), 1)
    spread = iota((LANES, PACKED), 1)
    target = lax.axis_index("pitch") * SLOT_LANES + lax.bitwise_and(there, SLOT_LANES - 1)
    slot_code = jnp.zeros((1, LANES), jnp.int32)
    hits = []
    for block in range(MODES // LANES):
        dest_col = column(dest_row, block)
        before = jnp.zeros((LANES, LANES), f32)
        for past in range(block + 1):
            same = dest_col == dest_row[:, past * LANES : (past + 1) * LANES]
            if past == block:
                same = same & (there < here)
            before = before + same.astype(f32)
        rank = jnp.sum(before, axis=1, keepdims=True).astype(jnp.int32)
        slot = dest_col * SLOT_LANES + rank
        hits.append(jnp.where(slot[:, :1] == spread, 1.0, 0.0).astype(bf16))
        mine = jnp.where(slot == target, column(code_row, block), 0)
        slot_code = slot_code + jnp.sum(mine, axis=0, keepdims=True)
    hit = jnp.concatenate(hits, axis=0)
    code_table = codes[source]
    lane_code = jnp.concatenate([column(code_table[0:1], g) for g in range(GROUPS)], axis=0)
    listed_at = (lane_code[:, :1] == code_row).astype(f32).astype(bf16)
    place[...] = jnp.dot(listed_at, hit, preferred_element_type=f32).astype(bf16)
    n = lax.shift_right_logical(slot_code, 7)
    m = n * own - (lax.bitwise_and(slot_code, 127) - K_MAX) * other
    m = jnp.where(n > 0, m, 0)
    wave = lax.bitwise_and(m + PITCH // 2, PITCH - 1) - PITCH // 2
    sigma = OMEGA * n.astype(f32) * own.astype(f32)
    kappa = KAPPA * wave.astype(f32) / PITCH
    lane = iota((1, LANES), 1)
    sign = jnp.where(lane < SLOT_LANES, -1.0, 1.0)
    terms[...] = jnp.zeros(terms.shape, f32)
    terms[0:1] = sign * sigma
    terms[1:2] = sign * kappa
    terms[2:3] = RELAX / (4.0 + sigma * sigma)
    for fetch in fetches:
        fetch.wait()


def spectrum_kernel(cells, weights, place, *rest):
    out, values = rest[-2:]
    lane = iota((8, LANES), 1)
    sub = iota((8, LANES), 0)
    parts = []
    for half in range(2):
        first = [ROWS_EACH * p + 4 * half for p in range(N_PITCH)]
        x = [cells[at : at + 8] for at in first]
        z = [x[p] + x[p + 16] for p in range(16)]
        even = [None] + [z[p] + z[16 - p] for p in range(1, 8)]
        odd = [None] + [z[p] - z[16 - p] for p in range(1, 8)]
        columns = []
        for t in range(9):
            re = z[0] + z[8] if t % 2 == 0 else z[0] - z[8]
            im = jnp.zeros((8, LANES), f32)
            for p in range(1, 8):
                re = re + math.cos(2.0 * math.pi * ((t * p) % 16) / 16) * even[p]
                if t % 8:
                    im = im - math.sin(2.0 * math.pi * ((t * p) % 16) / 16) * odd[p]
            columns.append((re, im))
        parts.append(columns)

    def edge(value, half, offset):
        spread = jnp.broadcast_to(value[6:7, :], (8, LANES))
        own = lane == sub + (offset + 4 * half)
        return jnp.sum(jnp.where(own, spread, 0.0), axis=1, keepdims=True)

    closed = []
    for half in range(2):
        columns = []
        for t in range(9):
            re, im = parts[half][t]
            edge_re, edge_im = parts[1][t]
            cos, sin = math.cos(2.0 * math.pi * t / 16), math.sin(2.0 * math.pi * t / 16)
            low_re, high_re = edge(edge_re, half, 0), edge(edge_re, half, 16)
            low_im, high_im = 0.0, 0.0
            if t % 8:
                low_im, high_im = edge(edge_im, half, 0), edge(edge_im, half, 16)
            re = re + jnp.where(lane == LANES - 1, cos * low_re - sin * low_im, 0.0)
            re = re + jnp.where(lane == 0, cos * high_re + sin * high_im, 0.0)
            im = im + jnp.where(lane == LANES - 1, cos * low_im + sin * low_re, 0.0)
            im = im + jnp.where(lane == 0, cos * high_im - sin * high_re, 0.0)
            columns += [re, im]
        closed.append(columns)
    wide = iota((16, LANES), 1)
    spot = lax.bitwise_and(wide, SLOT_LANES - 1)
    side = jnp.where(spot < HALF_CLASS, 1.0, -1.0)
    for group in range(GROUPS):
        re_lanes = jnp.zeros((16, LANES), f32)
        im_lanes = jnp.zeros((16, LANES), f32)
        for member in range(3):
            t = group * 3 + member
            left = jnp.concatenate(
                [closed[0][2 * t], closed[1][2 * t], closed[0][2 * t + 1], closed[1][2 * t + 1]], axis=0
            )
            high = left.astype(bf16)
            low = (left - high.astype(f32)).astype(bf16)
            both = jnp.dot(
                jnp.concatenate([high, low], axis=0), weights[0, t], preferred_element_type=f32
            )
            value = both[:32] + both[32:]
            value = value + jnp.dot(high, weights[1, t], preferred_element_type=f32)
            of_re, of_im = value[:16], pltpu.roll(value[16:], SLOT_LANES, 1)
            re = jnp.where(wide < SLOT_LANES, of_re, -of_re) + side * of_im
            im = pltpu.roll(re, SLOT_LANES, 1)
            first = member * CLASS_LANES
            if first:
                re, im = pltpu.roll(re, first, 1), pltpu.roll(im, first, 1)
            own = (wide >= first) & (wide < first + CLASS_LANES)
            re_lanes = jnp.where(own, re, re_lanes)
            im_lanes = jnp.where(own, im, im_lanes)
        values[0:16, group * LANES : (group + 1) * LANES] = re_lanes
        values[16:32, group * LANES : (group + 1) * LANES] = im_lanes
    x = values[...]
    high = x.astype(bf16)
    low = (x - high.astype(f32)).astype(bf16)
    split = jnp.concatenate([high, low], axis=0)
    lane = iota((8, LANES), 1)
    for block in range(N_PITCH // 4):
        picked = jnp.dot(
            split, place[:, 2 * block * LANES : 2 * (block + 1) * LANES], preferred_element_type=f32
        )
        picked = picked[0:32] + picked[32:64]
        for pair in range(2):
            here = picked[:, pair * LANES : (pair + 1) * LANES]
            at = ROWS_EACH * (4 * block + 2 * pair)
            for half in range(2):
                re, im = here[half * 8 : half * 8 + 8], here[16 + half * 8 : 24 + half * 8]
                spot = at + 4 * half
                out[spot : spot + 8] = jnp.where(lane < SLOT_LANES, re, pltpu.roll(im, SLOT_LANES, 1))
                spot = spot + ROWS_EACH
                out[spot : spot + 8] = jnp.where(lane < SLOT_LANES, pltpu.roll(re, SLOT_LANES, 1), im)


SPAN = RAD + 8


def turned(value):
    return pltpu.roll(value, SLOT_LANES, 1)


def swept(start, inside, jac, terms):
    length = start[0].shape[0]
    sigma, kappa, scale = terms[0:1], terms[1:2], terms[2:3]
    start = [w * inside for w in start]
    current = start
    for _ in range(2):
        above = [pltpu.roll(w, length - 1, 0) for w in current]
        below = [pltpu.roll(w, 1, 0) for w in current]
        grade = [above[f] - below[f] for f in range(F)]
        update = []
        for g in range(F):
            w = current[g]
            applied = 2.0 * w - 0.5 * (above[g] + below[g]) + sigma * turned(w)
            applied = applied + kappa * turned(mix(sweep_row(jac, 0, g), current))
            applied = applied + 0.5 * mix(sweep_row(jac, 1, g), grade)
            rest = start[g] - applied
            update.append((w + scale * (2.0 * rest - sigma * turned(rest))) * inside)
        current = update
    return current


def domain(radius):
    rad = lax.axis_index("rad")
    outside = ((radius < 0) & (rad == 0)) | ((radius >= RAD) & (rad == N_RAD - 1))
    return jnp.where(outside, 0.0, 1.0)


def beyond(modes, f):
    index = iota((8, LANES), 0)
    at = [ROWS_EACH * d + 11 for d in (f, F + f)]
    before = jnp.where(index == 7, modes[at[0] : at[0] + 1], 0.0)
    after = jnp.where(index == 0, modes[at[1] : at[1] + 1], 0.0)
    return before, after


def sweep_kernel(jac, modes, terms, after, main, near, far, body):
    inside = domain(iota((RAD + 16, LANES), 0) - 8)
    rad_even = lax.rem(lax.axis_index("rad"), 2) == 0
    start = []
    for f in range(F):
        low, high = beyond(modes, f)
        for side in range(2):
            body[f, pl.ds(side, N_PITCH, 2), :] = modes[pl.ds(side * F + f, N_PITCH, ROWS_EACH), :]
        start.append(jnp.concatenate([low, body[f], high], axis=0))
    for f, w in enumerate(swept(start, inside, jac, terms)):
        main[f] = w[8 : 8 + RAD]
        near[f] = jnp.where(rad_even, w[8 + RAD :], w[:8])
        far[f] = jnp.where(rad_even, w[:8], w[8 + RAD :])


def finish_kernel(main, near, far, out):
    index = iota((8, LANES), 0)
    rad_even = lax.rem(lax.axis_index("rad"), 2) == 0
    for f in range(F):
        from_low = jnp.where(rad_even, far[f], near[f])
        from_high = jnp.where(rad_even, near[f], far[f])
        first = main[f, 0:8] + jnp.where(index < 3, from_low, 0.0)
        last = main[f, RAD - 8 :] + jnp.where(index > 4, from_high, 0.0)
        body = jnp.concatenate([first, main[f, 8 : RAD - 8], last], axis=0)
        turned = jnp.transpose(body)
        out[pl.ds(2 * f, CAPACITY, 2 * F), :] = turned[:CAPACITY]
        out[pl.ds(2 * f + 1, CAPACITY, 2 * F), :] = turned[SLOT_LANES : SLOT_LANES + CAPACITY]


def shape(*dims, dtype=f32):
    return jax.ShapeDtypeStruct(dims, dtype)


def cost(flops, size):
    return pl.CostEstimate(flops=flops, bytes_accessed=size, transcendentals=0)


BIG = pltpu.CompilerParams(vmem_limit_bytes=20 * 1024 * 1024)


ANY = pl.BlockSpec(memory_space=pl.ANY)


def swap_pairs(count, first, periodic):
    pairs = []
    for i in range(first, count, 2):
        other = (i + 1) % count
        if other > i or periodic:
            pairs += [(i, other), (other, i)]
    return pairs


def transposed(value):
    value = value.reshape(SENT // 4, 4, LANES)
    return lax.all_to_all(value, "pitch", 0, 0, tiled=True).reshape(SENT, LANES)


def across(pairs):
    return [(row * N_RAD + i, (1 - row) * N_RAD + j) for row in range(2) for i, j in pairs]


def on_device(flow, inflow, flux_jacobian, sweep_jacobian, mode_index, destination):
    weights, codes = fourier_tables()
    flux_jac = jnp.transpose(flux_jacobian, (1, 2, 0, 3))
    near_pitch, far_pitch = swap_pairs(N_PITCH, 0, True), swap_pairs(N_PITCH, 1, True)
    near_rad, far_rad = swap_pairs(N_RAD, 0, False), swap_pairs(N_RAD, 1, False)

    pinned = pltpu.with_memory_space_constraint(flow, pltpu.HBM)

    face = pl.pallas_call(
        exit_kernel,
        out_shape=shape(SENT, LANES),
        in_specs=[ANY, ANY],
        out_specs=VMEM,
        scratch_shapes=[
            pltpu.VMEM((F, 2, RAD, LANES), f32),
            pltpu.SMEM((3, F, 1, F), f32),
            pltpu.VMEM((F, RAD, LANES), f32),
            pltpu.VMEM((RAD, LANES), f32),
            pltpu.SemaphoreType.DMA((F + 1,)),
        ],
        compiler_params=BIG,
        cost_estimate=cost(4_000_000, 600_000),
    )(pltpu.with_memory_space_constraint(flux_jac, pltpu.HBM), pinned)
    cells = transposed(face)

    faces = pl.pallas_call(
        halo_kernel,
        out_shape=(shape(RAD, LANES), shape(RAD, LANES), shape(F, AXIAL, LANES), shape(F, AXIAL, LANES)),
        in_specs=[VMEM],
        out_specs=(VMEM,) * 4,
        compiler_params=BIG,
        cost_estimate=cost(4_000_000, 1_400_000),
    )(flow)
    pitch_near = lax.ppermute(faces[0], "pitch", near_pitch)
    pitch_far = lax.ppermute(faces[1], "pitch", far_pitch)
    place, terms, own_weights = pl.pallas_call(
        table_kernel,
        out_shape=(
            shape(TABLE, PACKED, dtype=bf16),
            shape(8, LANES),
            shape(2, 9, LANES, LANES, dtype=bf16),
        ),
        in_specs=[VMEM, VMEM, VMEM, ANY],
        out_specs=(VMEM,) * 3,
        scratch_shapes=[pltpu.SemaphoreType.DMA((2,))],
        compiler_params=BIG,
        cost_estimate=cost(2 * TABLE * MODES * PACKED, 2_000_000),
    )(
        jnp.swapaxes(destination, 1, 2),
        mode_index,
        codes,
        pltpu.with_memory_space_constraint(jnp.asarray(weights), pltpu.HBM),
    )

    placed = pl.pallas_call(
        spectrum_kernel,
        out_shape=shape(SENT, LANES),
        in_specs=[VMEM, VMEM, VMEM, ANY, ANY],
        out_specs=VMEM,
        scratch_shapes=[pltpu.VMEM((32, TABLE), f32)],
        compiler_params=BIG,
        cost_estimate=cost(200_000_000, 3_000_000),
    )(
        cells,
        own_weights,
        place,
        pitch_near,
        pitch_far,
    )
    amplitude = transposed(placed)

    sweep_jac = jnp.transpose(sweep_jacobian, (0, 2, 1, 3))
    *rows, sweep_jac = lax.optimization_barrier((faces[2], faces[3], sweep_jac, placed))[:3]
    sweep_jac = lax.ppermute(sweep_jac, "row", [(0, 1), (1, 0)])
    rad_near = lax.ppermute(rows[0], "rad", near_rad)
    rad_far = lax.ppermute(rows[1], "rad", far_rad)
    next_flow, flux_done = pl.pallas_call(
        flux_kernel,
        grid=(AXIAL // DEPTH,),
        out_shape=(shape(1, F, AXIAL, RAD, LANES), shape(8, LANES)),
        in_specs=[
            SMEM,
            pl.BlockSpec((1, F, DEPTH, RAD, LANES), lambda z: (0, 0, z, 0, 0)),
            pl.BlockSpec((1, F, RAD, LANES), lambda z: (0, 0, 0, 0)),
            pl.BlockSpec((RAD, LANES), lambda z: (0, 0)),
            pl.BlockSpec((RAD, LANES), lambda z: (0, 0)),
            pl.BlockSpec((F, AXIAL, LANES), lambda z: (0, 0, 0)),
            pl.BlockSpec((F, AXIAL, LANES), lambda z: (0, 0, 0)),
            ANY,
        ],
        out_specs=(
            pl.BlockSpec((1, F, DEPTH, RAD, LANES), lambda z: (0, 0, z, 0, 0)),
            pl.BlockSpec((8, LANES), lambda z: (0, 0)),
        ),
        scratch_shapes=[pltpu.VMEM((F, RAD, LANES), f32)],
        compiler_params=BIG,
        cost_estimate=cost(20_000_000, 3_000_000),
    )(flux_jac, pinned, inflow, pitch_near, pitch_far, rad_near, rad_far, placed)

    main, near, far = pl.pallas_call(
        sweep_kernel,
        out_shape=(shape(F, RAD, LANES), shape(F, 8, LANES), shape(F, 8, LANES)),
        in_specs=[SMEM, VMEM, VMEM, ANY],
        out_specs=(VMEM,) * 3,
        scratch_shapes=[pltpu.VMEM((F, RAD, LANES), f32)],
        compiler_params=BIG,
        cost_estimate=cost(8_000_000, 500_000),
    )(sweep_jac, amplitude, terms, flux_done)
    near = lax.ppermute(near, ("row", "rad"), across(near_rad))
    far = lax.ppermute(far, ("row", "rad"), across(far_rad))
    main = lax.ppermute(main, "row", [(0, 1), (1, 0)])
    response = pl.pallas_call(
        finish_kernel,
        out_shape=shape(CAPACITY * F * 2, RAD),
        in_specs=[VMEM] * 3,
        out_specs=VMEM,
        compiler_params=BIG,
        cost_estimate=cost(1_000_000, 800_000),
    )(main, near, far)
    response = response.reshape(1, 1, CAPACITY, F, 2, RAD)
    return next_flow, jnp.swapaxes(response, 3, 4)


def solution(mesh):
    placed = (
        P("row", None, None, "rad", "pitch"),
        P("row", None, "rad", "pitch"),
        P("row", None, None, None),
        P("row", None, None, None),
        P(),
        P(),
    )
    return jax.shard_map(
        on_device,
        mesh=mesh,
        in_specs=placed,
        out_specs=(
            P("row", None, None, "rad", "pitch"),
            P("row", "pitch", None, None, None, "rad"),
        ),
        check_vma=False,
    )
```
